128 devices in a mesh: section: 2 (over y_hi), dp: 16 (over x, y_lo, core), tensor: 4 (over z).
Axes of the slice: x: 4, y: 4 (y_hi: 2, y_lo: 2; y = y_hi * 2 + y_lo), z: 4, core: 2. Of those that a mesh axis runs over, the one named last changes fastest.
Arguments:
- inputs: bfloat16 [2, 4096, 1024], P(None, ('dp', 'tensor')), may hold values from -6 to 6
- cotangent: bfloat16 [2, 4096, 1024], P(None, ('dp', 'tensor')), may hold values from -6 to 6
- segments: int32 [2, 16, 256], P(None, 'dp'), may hold values from 0 to 3, as said below
- qkv_weight: bfloat16 [2, 1024, 3, 1024], P('section', 'dp', None, 'tensor'), may hold values from -0.25 to 0.25
- out_weight: bfloat16 [2, 1024, 1024], P('section', 'tensor', 'dp'), may hold values from -0.5 to 0.5
- fc1_weight: bfloat16 [2, 1024, 4096], P('section', 'dp', 'tensor'), may hold values from -0.1875 to 0.1875
- fc2_weight: bfloat16 [2, 4096, 1024], P('section', 'tensor', 'dp'), may hold values from -0.09375 to 0.09375
- ln_gains: float32 [2, 2, 1024], P('section'), may hold values from 0.25 to 1.75
- ln_biases: float32 [2, 2, 1024], P('section'), may hold values from -2.5 to 2.5
- qv_bias: float32 [2, 2, 1024], P('section'), may hold values from -2.5 to 2.5
- proj_biases: float32 [2, 2, 1024], P('section'), may hold values from -2.5 to 2.5
- fc_bias: float32 [2, 4096], P('section'), may hold values from -2.5 to 2.5
Outputs:
- section_outputs: float32 [2, 2, 4096, 1024], P('section', None, ('dp', 'tensor'))
- section_grads: float32 [2, 2, 4096, 1024], P('section', None, ('dp', 'tensor'))
- qkv_grad: float32 [2, 1024, 3, 1024], P('section', 'dp', None, 'tensor')
- out_grad: float32 [2, 1024, 1024], P('section', 'tensor', 'dp')
- fc1_grad: float32 [2, 1024, 4096], P('section', 'dp', 'tensor')
- fc2_grad: float32 [2, 4096, 1024], P('section', 'tensor', 'dp')
- gain_grad: float32 [2, 2, 1024], P('section')
- offset_grad: float32 [2, 2, 1024], P('section')
- qv_bias_grad: float32 [2, 2, 1024], P('section')
- proj_bias_grad: float32 [2, 2, 1024], P('section')
- fc_bias_grad: float32 [2, 4096], P('section')
The draws below stay inside these ranges and needn't reach their ends.
Inputs may be any that keep to these rules, and one draw needn't show every extreme that they name: `segments`: in every row of 256 tokens the ids run 0, 1, 2, 3 in order, never falling, each present; document 1 starts within the row's first 64 tokens and ends within its last 64 tokens.
All inputs are finite; a program needn't handle non-finite values.
Results may differ from the reference program's by a relative error of at most 0.02.
Values may be sent and summed in bfloat16 or wider, within the bound.
A program may use at most 128 MiB of HBM per device.

```python
import math
import jax
import jax.numpy as jnp
from jax import lax

D = 1024
HEADS = 16
HD = 64
FF = 4096
SEQ = 256
MICRO = 2
GROUPS = 16
SEQ_DEV = 64
TOKENS = 4096


def draw_segments(key, part):
    key = jax.random.fold_in(key, 11)
    first_key, second_key, third_key = jax.random.split(key, 3)
    row_shape = (MICRO, GROUPS, 1)
    start_cut = jax.random.randint(first_key, row_shape, 1, SEQ_DEV)
    end_cut = jax.random.randint(second_key, row_shape, SEQ - SEQ_DEV + 1, SEQ - 1)
    last_cut = jax.random.randint(third_key, row_shape, end_cut + 1, SEQ)
    places = jnp.arange(SEQ, dtype=jnp.int32)[None, None, :]
    return (places >= start_cut).astype(jnp.int32) + (places >= end_cut).astype(jnp.int32) + (places >= last_cut).astype(jnp.int32)


def steps_of(own_key, dims, cuts, least, high):
    factor_of, own = 1.0, jax.random.fold_in(own_key, 6)
    for axis_at, blocks in cuts:
        heights = jnp.exp(jax.random.uniform(jax.random.fold_in(own, axis_at), (blocks,), jnp.float32, least / len(cuts), high / len(cuts)))
        factor_of = factor_of * jnp.repeat(heights, dims[axis_at] // blocks).reshape([-1 if axis == axis_at else 1 for axis in range(len(dims))])
    return factor_of


def gaussian(rng, extent, deviation, limit, cuts=(), kind=jnp.bfloat16):
    array = jax.random.normal(rng, extent, jnp.float32) * deviation
    if len(cuts) > 0:
        array = steps_of(rng, extent, cuts, -0.22, 0.18) * array
    return jnp.clip(array, min=-limit, max=limit).astype(kind)


def setup_inputs(seed: int = 0) -> dict:
    seeds = jax.random.split(jax.random.key(seed), 13)
    inputs = gaussian(seeds[0], (MICRO, TOKENS, D), 1.0, 6.0, ((1, 64),))
    cotangent = gaussian(seeds[1], (MICRO, TOKENS, D), 1.0, 6.0, ((1, 64),))
    segments = draw_segments(jax.random.fold_in(seeds[12], 71), 0)
    qkv_weight = gaussian(seeds[3], (2, D, 3, D), (D // 2) ** -0.5, 0.25, ((0, 2), (1, 16), (3, 4)))
    out_weight = gaussian(seeds[4], (2, D, D), (D * 32 // SEQ) ** -0.5, 0.5, ((0, 2), (1, 4), (2, 16)))
    fc1_weight = gaussian(seeds[5], (2, D, FF), D ** -0.5, 0.1875, ((0, 2), (1, 16), (2, 4)))
    fc2_weight = gaussian(seeds[6], (2, FF, D), FF ** -0.5, 0.09375, ((0, 2), (1, 4), (2, 16)))
    ln_gains = jnp.clip(1.0 + 0.15 * jax.random.normal(seeds[7], (2, 2, D), jnp.float32), 0.25, 1.75)
    ln_biases = gaussian(seeds[8], (2, 2, D), 0.3, 2.5, ((0, 2),), jnp.float32)
    qv_bias = gaussian(seeds[9], (2, 2, D), 0.3, 2.5, ((0, 2),), jnp.float32)
    proj_biases = gaussian(seeds[10], (2, 2, D), 0.3, 2.5, ((0, 2),), jnp.float32)
    fc_bias = gaussian(seeds[11], (2, FF), 0.3, 2.5, ((0, 2),), jnp.float32)
    return dict(inputs=inputs, cotangent=cotangent, segments=segments, qkv_weight=qkv_weight, out_weight=out_weight, fc1_weight=fc1_weight, fc2_weight=fc2_weight, ln_gains=ln_gains, ln_biases=ln_biases, qv_bias=qv_bias, proj_biases=proj_biases, fc_bias=fc_bias)


@jax.custom_vjp
def low(v):
    return lax.optimization_barrier(v.astype(jnp.bfloat16)).astype(jnp.float32)

@jax.custom_vjp
def low_back(v):
    return v

def low_keep(v):
    return (low(v), None)

def low_pass(kept, grad):
    return (grad,)

def back_keep(v):
    return (v, None)

def back_low(kept, grad):
    return (low(grad),)
low.defvjp(low_keep, low_pass)
low_back.defvjp(back_keep, back_low)
NEGATIVE = -1000000000.0
GELU_COEF = 0.7978845608028654

def matmul_high(left_side, right_side):
    return jnp.dot(left_side, right_side, precision=lax.Precision.HIGHEST, preferred_element_type=jnp.float32)

def norm_rows(hidden, gain_row, offset_row):
    centre = hidden - lax.optimization_barrier(jnp.mean(hidden, axis=-1, keepdims=True))
    spread = lax.optimization_barrier(jnp.mean(centre * centre, axis=-1, keepdims=True))
    return centre * lax.rsqrt(spread + 1e-05) * gain_row + offset_row

def gelu_tanh(values):
    return 0.5 * values * (1.0 + jnp.tanh(GELU_COEF * (values + 0.044715 * values * values * values)))

def layer_forward(hidden, seg_row, qkv_weight, out_weight, fc1_weight, fc2_weight, gain_rows, offset_rows, qv_bias, proj_biases, fc_bias):
    seq_len = hidden.shape[0]
    scale_factor = 1.0 / math.sqrt(HD)
    first_normed = low(norm_rows(hidden, gain_rows[0], offset_rows[0]))
    projected = matmul_high(first_normed, qkv_weight.reshape(D, 3 * D)).reshape(seq_len, 3, D)
    queries = low(low_back(projected[:, 0]) + qv_bias[0])
    key_rows = low(low_back(projected[:, 1]))
    value_rows = low(low_back(projected[:, 2]) + qv_bias[1])
    places = jnp.arange(seq_len)
    allowed = (seg_row[:, None] == seg_row[None, :]) & (places[:, None] >= places[None, :])
    query_heads = queries.reshape(seq_len, HEADS, HD)
    key_heads = key_rows.reshape(seq_len, HEADS, HD)
    value_heads = value_rows.reshape(seq_len, HEADS, HD)
    scores = jnp.einsum('qhd,khd->hqk', query_heads, key_heads, precision=lax.Precision.HIGHEST) * scale_factor
    scores = low_back(jnp.where(allowed[None], scores, NEGATIVE))
    row_max = lax.optimization_barrier(jnp.max(scores, axis=-1, keepdims=True))
    shifted = jnp.exp(scores - row_max)
    attn_probs = shifted / lax.optimization_barrier(jnp.sum(shifted, axis=-1, keepdims=True))
    mixed_rows = jnp.einsum('hqk,khd->qhd', low(attn_probs), value_heads, precision=lax.Precision.HIGHEST).reshape(seq_len, D)
    mixed_rows = low_back(low(mixed_rows))
    middle = hidden + (low_back(matmul_high(mixed_rows, out_weight)) + proj_biases[0])
    second_normed = low(norm_rows(middle, gain_rows[1], offset_rows[1]))
    before = low_back(matmul_high(second_normed, fc1_weight)) + fc_bias
    active = low(gelu_tanh(before))
    return middle + (low_back(matmul_high(active, fc2_weight)) + proj_biases[1])

def two_sections(row_value, mid_shift, seg_row, params):
    first_out = layer_forward(row_value, seg_row, *[member[0] for member in params])
    second_in = low_back(low(first_out) + mid_shift)
    last_out = layer_forward(second_in, seg_row, *[member[1] for member in params])
    return (last_out, first_out)

def reference(inputs, cotangent, segments, qkv_weight, out_weight, fc1_weight, fc2_weight, ln_gains, ln_biases, qv_bias, proj_biases, fc_bias):
    weights = tuple((member.astype(jnp.float32) for member in (qkv_weight, out_weight, fc1_weight, fc2_weight, ln_gains, ln_biases, qv_bias, proj_biases, fc_bias)))
    row_count = MICRO * GROUPS
    rows_in = inputs.astype(jnp.float32).reshape(row_count, SEQ, D)
    rows_cot = cotangent.astype(jnp.float32).reshape(row_count, SEQ, D)
    rows_seg = segments.reshape(row_count, SEQ)

    def one_row(totals, row_item):
        row_in, row_cot, row_seg = row_item

        def run_rows(row_value, mid_shift, params):
            return two_sections(row_value, mid_shift, row_seg, params)
        last_out, pull_back, first_out = jax.vjp(run_rows, row_in, jnp.zeros_like(row_in), weights, has_aux=True)
        grad_in, grad_mid, grad_weights = pull_back(row_cot)
        totals = jax.tree.map(jnp.add, totals, grad_weights)
        return (totals, (first_out, last_out, grad_in, grad_mid))
    zero_grads = jax.tree.map(jnp.zeros_like, weights)
    totals, outs_rows = lax.scan(one_row, zero_grads, (rows_in, rows_cot, rows_seg))
    first_rows, last_rows, in_grads, mid_grads = outs_rows
    out_shape = (MICRO, TOKENS, D)
    section_outputs = jnp.stack([first_rows.reshape(out_shape), last_rows.reshape(out_shape)])
    section_grads = jnp.stack([in_grads.reshape(out_shape), mid_grads.reshape(out_shape)])
    return (section_outputs, section_grads, totals[0], totals[1], totals[2], totals[3], totals[4], totals[5], totals[6], totals[7], totals[8])
```

```python
import functools
import math

import jax
import jax.numpy as jnp
from jax import lax
from jax.experimental import pallas as pl
from jax.experimental.pallas import tpu as pltpu
from jax.sharding import PartitionSpec as P

D = 1024
HD = 64
FF = 4096
SEQ = 256
ROWS = 64
WIDE = 3072
NEGATIVE = -1000000000.0
GELU_COEF = 0.7978845608028654
EPSILON = 1e-05
MESH = pl.DeviceIdType.MESH
BF16 = jnp.bfloat16
F32 = jnp.float32

GAIN, OFFSET, PROJ, QV, FC = 0, 2, 4, 6, 8
SMALL = 16


def dot_nn(a, b):
    return lax.dot_general(a, b, (((1,), (0,)), ((), ())), preferred_element_type=F32)


def dot_nt(a, b):
    return lax.dot_general(a, b, (((1,), (1,)), ((), ())), preferred_element_type=F32)


def dot_tn(a, b):
    return lax.dot_general(a, b, (((0,), (0,)), ((), ())), preferred_element_type=F32)


def norm_rows(hidden, gain_row, offset_row):
    centre = hidden - jnp.mean(hidden, axis=-1, keepdims=True)
    spread = jnp.mean(centre * centre, axis=-1, keepdims=True)
    inverse = lax.rsqrt(spread + EPSILON)
    unit_rows = centre * inverse
    return unit_rows * gain_row + offset_row, unit_rows, inverse


def norm_back(grad_rows, unit_rows, inverse, gain_row):
    grad_unit = grad_rows * gain_row
    return inverse * (
        grad_unit
        - jnp.mean(grad_unit, axis=-1, keepdims=True)
        - unit_rows * jnp.mean(grad_unit * unit_rows, axis=-1, keepdims=True)
    )


def row_sum(value):
    return jnp.sum(value, axis=0, keepdims=True)


def kernel(
    x_ref, cot_ref, seg_ref, shard_ref, gain_ref, offset_ref, qv_ref, proj_ref, fc_ref,
    out_ref, grad_ref, wgrad_ref, small_ref,
    w, gd, r0, r1, r2, p1, pb,
    g1, g2, gm, ga, sbuf, rbuf,
    qkv_s, prob_s, mixed_s, active_s, slope_s, unit_s, inv_s, mid_s,
    gb_s, gp_s, gt_s, mask_s, dy_s, xs, xr, sm, arm, arx, ary, arz,
    z_send, z_recv, gy_send, gy_recv, gx_send, gx_recv, gc_send, gc_recv,
    rc_send, rc_recv, rx_send, rx_recv, ry_send, ry_recv, o_send, o_recv, a_send, a_recv,
):
    s = lax.axis_index("section")
    d = lax.axis_index("dp")
    t = lax.axis_index("tensor")
    x = d // 4
    yl = (d // 2) % 2
    c = d % 2
    y = 2 * s + yl
    mate = {"section": s, "dp": d + 1 - 2 * c, "tensor": t}
    zp = [{"section": s, "dp": d, "tensor": (t + k) % 4} for k in (1, 2, 3)]
    xp = [{"section": s, "dp": ((x + k) % 4) * 4 + yl * 2 + c, "tensor": t} for k in (1, 2, 3)]
    yp = []
    for k in (1, 2, 3):
        other = (y + k) % 4
        yp.append({"section": other // 2, "dp": x * 4 + (other % 2) * 2 + c, "tensor": t})
    across = {"section": 1 - s, "dp": d, "tensor": t}

    def remote(src, dst, send, recv, peer):
        return pltpu.make_async_remote_copy(
            src_ref=src, dst_ref=dst, send_sem=send, recv_sem=recv, device_id=peer, device_id_type=MESH
        )

    pending = {}

    def begin(key, copy, cond=None):
        if cond is None:
            copy.start()
        else:
            pl.when(cond)(copy.start)
        pending.setdefault(key, []).append((copy, cond))

    def flush(key):
        for copy, cond in pending.pop(key, []):
            if cond is None:
                copy.wait_send()
            else:
                pl.when(cond)(copy.wait_send)

    barrier = pltpu.get_barrier_semaphore()
    for peer in zp + xp + yp + [mate]:
        pl.semaphore_signal(barrier, inc=1, device_id=peer, device_id_type=MESH)
    pl.semaphore_wait(barrier, 10)

    def cols(g):
        return pl.ds(g * 1024, 1024)

    def gather_y(g):
        for k in (1, 2, 3):
            begin("gy", remote(
                shard_ref.at[:, cols(g)], w.at[s, 2 * x + yl, c, :, cols(g)],
                gy_send.at[g, k - 1], gy_recv.at[s, g, k - 1], yp[k - 1],
            ))

    def gather_x(l, g):
        for k in (1, 2, 3):
            src_y = (y - k + 4) % 4
            copy = remote(
                shard_ref.at[:, cols(g)], w.at[l, 2 * x + src_y % 2, c, :, cols(g)],
                gy_send.at[g, k - 1], gy_recv.at[l, g, k - 1], yp[k - 1],
            )
            pl.when(src_y // 2 == l)(copy.wait_recv)
        mine = w.at[l, pl.ds(2 * x, 2), c, :, cols(g)]
        for k in (1, 2, 3):
            begin("gx", remote(mine, mine, gx_send.at[l, g, k - 1], gx_recv.at[l, g, k - 1], xp[k - 1]))

    def gather_c(l, g):
        for k in (1, 2, 3):
            theirs = w.at[l, pl.ds(2 * ((x - k + 4) % 4), 2), c, :, cols(g)]
            remote(theirs, theirs, gx_send.at[l, g, k - 1], gx_recv.at[l, g, k - 1], xp[k - 1]).wait_recv()
        half = w.at[l, :, c, :, cols(g)]
        begin("gc", remote(half, half, gc_send.at[l, g], gc_recv.at[l, g], mate))

    def gather_done(l, g):
        half = w.at[l, :, 1 - c, :, cols(g)]
        remote(half, half, gc_send.at[l, g], gc_recv.at[l, g], mate).wait_recv()

    def reduce_c(l, g):
        begin(("rc", l, g), remote(
            gd.at[:, 1 - c, :, cols(g)], r0.at[l, :, :, cols(g)], rc_send.at[l, g], rc_recv.at[l, g], mate
        ))

    def reduce_x(l, g):
        remote(
            gd.at[:, 1 - c, :, cols(g)], r0.at[l, :, :, cols(g)], rc_send.at[l, g], rc_recv.at[l, g], mate
        ).wait_recv()

        def add(i, _):
            gd[i, c, :, cols(g)] = (
                gd[i, c, :, cols(g)].astype(F32) + r0[l, i, :, cols(g)].astype(F32)
            ).astype(BF16)
            return 0

        lax.fori_loop(0, 8, add, 0)
        for k in (1, 2, 3):
            begin(("rx", l, g), remote(
                gd.at[pl.ds(2 * ((x + k) % 4), 2), c, :, cols(g)], r1.at[l, k - 1, :, :, cols(g)],
                rx_send.at[l, g, k - 1], rx_recv.at[l, g, k - 1], xp[k - 1],
            ))

    def reduce_y(l, g):
        for k in (1, 2, 3):
            remote(
                gd.at[pl.ds(2 * ((x + k) % 4), 2), c, :, cols(g)], r1.at[l, k - 1, :, :, cols(g)],
                rx_send.at[l, g, k - 1], rx_recv.at[l, g, k - 1], xp[k - 1],
            ).wait_recv()
        for half in (0, 1):
            total = gd[2 * x + half, c, :, cols(g)].astype(F32)
            for k in (0, 1, 2):
                total += r1[l, k, half, :, cols(g)].astype(F32)
            p1[l, half, :, cols(g)] = total.astype(BF16)
        for k in (1, 2, 3):
            target = (y + k) % 4
            begin("ry", remote(
                p1.at[l, target % 2, :, cols(g)], r2.at[l, k - 1, :, cols(g)],
                ry_send.at[l, g, k - 1], ry_recv.at[l, g, k - 1], yp[k - 1],
            ), target // 2 == l)

    def reduce_done(l, g):
        copies = [
            remote(
                p1.at[l, 0, :, cols(g)], r2.at[l, k, :, cols(g)],
                ry_send.at[l, g, k], ry_recv.at[l, g, k], yp[k],
            )
            for k in (0, 1, 2)
        ]

        @pl.when(s == l)
        def _():
            for copy in copies:
                copy.wait_recv()
            total = p1[l, yl, :, cols(g)].astype(F32)
            for k in (0, 1, 2):
                total += r2[l, k, :, cols(g)].astype(F32)
            wgrad_ref[:, cols(g)] = total

    def spread_start(event, buf):
        for k in (1, 2, 3):
            begin("z", remote(buf.at[t], buf.at[t], z_send.at[event, k - 1], z_recv.at[event, k - 1], zp[k - 1]))

    def spread_done(event, buf):
        for k in (1, 2, 3):
            theirs = buf.at[(t - k + 4) % 4]
            remote(theirs, theirs, z_send.at[event, k - 1], z_recv.at[event, k - 1], zp[k - 1]).wait_recv()

    def sum_start(event):
        slot = event % 2
        for k in (1, 2, 3):
            begin(("s", slot), remote(
                sbuf.at[slot, (t + k) % 4], rbuf.at[event, k - 1],
                z_send.at[event, k - 1], z_recv.at[event, k - 1], zp[k - 1],
            ))

    def sum_done(event):
        slot = event % 2
        for k in (1, 2, 3):
            remote(
                sbuf.at[slot, (t + k) % 4], rbuf.at[event, k - 1],
                z_send.at[event, k - 1], z_recv.at[event, k - 1], zp[k - 1],
            ).wait_recv()
        total = sbuf[slot, t].astype(F32)
        for k in (0, 1, 2):
            total += rbuf[event, k].astype(F32)
        return total

    def share(event, lhs, l, c0, n):
        slot = event % 2
        flush(("s", slot))

        def tile(j, _):
            right = w[l, pl.ds(2 * j, 2), :, :, pl.ds(c0, n)].reshape(256, n)
            part = dot_nt(lhs(), right).astype(BF16)
            sbuf[slot, :, :, pl.ds(pl.multiple_of(j * 256, 256), 256)] = part.reshape(4, 64, 256)
            return 0

        lax.fori_loop(0, 4, tile, 0)

    def weight_grad(lhs_ref, rhs, c0, n):
        def turn(i, _):
            piece = lhs_ref[:, :, pl.ds(pl.multiple_of(i * 256, 256), 256)].reshape(256, 256)
            gt_s[pl.ds(pl.multiple_of(i * 256, 256), 256), :] = piece.T
            return 0

        lax.fori_loop(0, 4, turn, 0)

        def tile(step, _):
            i, j = step // (n // 256), step % (n // 256)
            left = gt_s[pl.ds(pl.multiple_of(i * 256, 256), 256), :]
            part = dot_nn(left, rhs[:, pl.ds(pl.multiple_of(j * 256, 256), 256)])
            gd[pl.ds(2 * i, 2), :, :, pl.ds(pl.multiple_of(c0 + j * 256, 256), 256)] = part.astype(
                BF16
            ).reshape(2, 2, 64, 256)
            return 0

        lax.fori_loop(0, 4 * (n // 256), tile, 0)

    def cross_send(index, value, l, local_ref):
        @pl.when(s == l)
        def _():
            local_ref[s] = value

        @pl.when(s != l)
        def _():
            xs[index] = value

        begin("o", remote(xs.at[index], xr.at[index], o_send.at[index], o_recv.at[index], across), s != l)

    gather_y(0)
    pb[s, GAIN:GAIN + 2] = gain_ref[...]
    pb[s, OFFSET:OFFSET + 2] = offset_ref[...]
    pb[s, PROJ:PROJ + 2] = proj_ref[...]
    pb[s, QV:QV + 2] = qv_ref[...]
    for k in range(4):
        pb[s, FC + k:FC + k + 1] = fc_ref[:, k * 1024:(k + 1) * 1024]
    pb[s, FC + 4:] = jnp.zeros((SMALL - FC - 4, D), F32)
    begin("pb", remote(pb.at[s], pb.at[s], o_send.at[2], o_recv.at[2], across))
    gm[1, t] = cot_ref[s]
    spread_start(8, gm.at[1])
    w[s, 2 * x + yl, c] = shard_ref[...]
    sm[...] = jnp.zeros_like(sm)
    seg_rows = jnp.broadcast_to(seg_ref[s].astype(F32), (SEQ, SEQ))
    seg_cols = seg_rows.T
    places_i = lax.broadcasted_iota(jnp.int32, (SEQ, SEQ), 0)
    places_j = lax.broadcasted_iota(jnp.int32, (SEQ, SEQ), 1)
    mask_s[...] = jnp.where((seg_rows == seg_cols) & (places_i >= places_j), 1.0, 0.0)
    remote(pb.at[1 - s], pb.at[1 - s], o_send.at[2], o_recv.at[2], across).wait_recv()

    def small(l, row):
        return pb[l, row:row + 1]

    def forward(l, hidden, pump):
        normed, unit, inverse = norm_rows(hidden, small(l, GAIN), small(l, OFFSET))
        unit_s[l, 0] = unit
        inv_s[l, 0] = inverse
        g1[l, t] = normed.astype(BF16)
        spread_start(4 * l, g1.at[l])
        mid_s[...] = hidden
        pump(0)
        spread_done(4 * l, g1.at[l])
        gather_done(l, 0)
        for j in range(3):
            part = dot_nn(
                g1[l].reshape(SEQ, D), w[l, :, :, :, j * 256:(j + 1) * 256].reshape(D, 256)
            )
            if j != 1:
                part = part + pb[l, QV + j // 2:QV + j // 2 + 1, pl.ds(pl.multiple_of(t * 256, 256), 256)]
            qkv_s[l, :, j * 256:(j + 1) * 256] = part.astype(BF16)
        pump(1)
        for pair in range(2):
            mixed = []
            for n in (2 * pair, 2 * pair + 1):
                lo = n * HD
                scores = dot_nt(qkv_s[l, :, lo:lo + HD], qkv_s[l, :, 256 + lo:256 + lo + HD]) * 0.125
                scores = jnp.where(mask_s[...] > 0.5, scores, NEGATIVE)
                shifted = jnp.exp(scores - jnp.max(scores, axis=-1, keepdims=True))
                probs = shifted / jnp.sum(shifted, axis=-1, keepdims=True)
                prob_s[l, n] = probs
                mixed.append(dot_nn(probs.astype(BF16), qkv_s[l, :, 512 + lo:512 + lo + HD]))
            mixed_s[l, :, pair * 128:(pair + 1) * 128] = jnp.concatenate(mixed, axis=1).astype(BF16)
        share(4 * l + 1, lambda: mixed_s[l], l, 768, 256)
        sum_start(4 * l + 1)
        pump(2)
        middle = mid_s[...] + (sum_done(4 * l + 1) + small(l, PROJ))
        normed, unit, inverse = norm_rows(middle, small(l, GAIN + 1), small(l, OFFSET + 1))
        unit_s[l, 1] = unit
        inv_s[l, 1] = inverse
        g2[l, t] = normed.astype(BF16)
        spread_start(4 * l + 2, g2.at[l])
        mid_s[...] = middle
        pump(3)
        spread_done(4 * l + 2, g2.at[l])
        gather_done(l, 1)

        def up(j, _):
            at = pl.ds(pl.multiple_of(j * 256, 256), 256)
            before = dot_nn(
                g2[l].reshape(SEQ, D),
                w[l, :, :, :, pl.ds(pl.multiple_of(1024 + j * 256, 256), 256)].reshape(D, 256),
            ) + pb[l, pl.ds(FC + t, 1), at]
            tanh_part = jnp.tanh(GELU_COEF * (before + 0.044715 * before * before * before))
            active_s[l, :, at] = (0.5 * before * (1.0 + tanh_part)).astype(BF16)
            slope_s[l, :, at] = 0.5 * (1.0 + tanh_part) + 0.5 * before * (
                1.0 - tanh_part * tanh_part
            ) * GELU_COEF * (1.0 + 3.0 * 0.044715 * before * before)
            return 0

        lax.fori_loop(0, 4, up, 0)
        pump(4)
        gather_done(l, 2)
        share(4 * l + 3, lambda: active_s[l], l, 2048, 1024)
        sum_start(4 * l + 3)
        pump(5)
        return mid_s[...] + (sum_done(4 * l + 3) + small(l, PROJ + 1))

    def backward(l, pump):
        event = 8 + 4 * (1 - l)
        row = l * SMALL
        sm[row + PROJ + 1:row + PROJ + 2] = row_sum(dy_s[...])
        spread_done(event, gm.at[l])

        def down(j, _):
            at = pl.ds(pl.multiple_of(j * 256, 256), 256)
            grad_before = dot_nn(
                gm[l].reshape(SEQ, D),
                w[l, :, :, :, pl.ds(pl.multiple_of(2048 + j * 256, 256), 256)].reshape(D, 256),
            ) * slope_s[l, :, at]
            sm[pl.ds(row + FC + t, 1), at] = row_sum(grad_before)
            gb_s[:, at] = grad_before.astype(BF16)
            return 0

        lax.fori_loop(0, 4, down, 0)
        share(event + 1, lambda: gb_s[...], l, 1024, 1024)
        sum_start(event + 1)
        pump(0)
        weight_grad(gm.at[l], active_s.at[l], 2048, 1024)
        reduce_c(l, 2)
        weight_grad(g2.at[l], gb_s, 1024, 1024)
        reduce_c(l, 1)
        pump(1)
        grad = sum_done(event + 1)
        sm[row + GAIN + 1:row + GAIN + 2] = row_sum(grad * unit_s[l, 1])
        sm[row + OFFSET + 1:row + OFFSET + 2] = row_sum(grad)
        grad_middle = dy_s[...] + norm_back(grad, unit_s[l, 1], inv_s[l, 1], small(l, GAIN + 1))
        dy_s[...] = grad_middle
        ga[l, t] = grad_middle.astype(BF16)
        spread_start(event + 2, ga.at[l])
        sm[row + PROJ:row + PROJ + 1] = row_sum(grad_middle)
        pump(2)
        spread_done(event + 2, ga.at[l])
        grad_mixed = dot_nn(
            ga[l].reshape(SEQ, D), w[l, :, :, :, 768:1024].reshape(D, 256)
        ).astype(BF16)
        for pair in range(2):
            grads = [[], [], []]
            for n in (2 * pair, 2 * pair + 1):
                lo = n * HD
                q = qkv_s[l, :, lo:lo + HD]
                key = qkv_s[l, :, 256 + lo:256 + lo + HD]
                value = qkv_s[l, :, 512 + lo:512 + lo + HD]
                grad_head = grad_mixed[:, lo:lo + HD]
                probs = prob_s[l, n]
                grad_probs = dot_nt(grad_head, value)
                row_dot = jnp.sum(probs * grad_probs, axis=-1, keepdims=True)
                grad_scores = (probs * (grad_probs - row_dot)).astype(BF16)
                grads[0].append(dot_nn(grad_scores, key) * 0.125)
                grads[1].append(dot_tn(grad_scores, q) * 0.125)
                grads[2].append(dot_tn(probs.astype(BF16), grad_head))
            for j in range(3):
                both = jnp.concatenate(grads[j], axis=1)
                gp_s[:, j * 256 + pair * 128:j * 256 + (pair + 1) * 128] = both.astype(BF16)
                if j != 1:
                    sm[
                        row + QV + j // 2:row + QV + j // 2 + 1,
                        pl.ds(pl.multiple_of(t * 256 + pair * 128, 128), 128),
                    ] = row_sum(both)
        share(event + 3, lambda: gp_s[...], l, 0, 768)
        sum_start(event + 3)
        pump(3)
        weight_grad(ga.at[l], mixed_s.at[l], 768, 256)
        weight_grad(g1.at[l], gp_s, 0, 768)
        reduce_c(l, 0)
        pump(4)
        grad = sum_done(event + 3)
        sm[row + GAIN:row + GAIN + 1] = row_sum(grad * unit_s[l, 0])
        sm[row + OFFSET:row + OFFSET + 1] = row_sum(grad)
        return dy_s[...] + norm_back(grad, unit_s[l, 0], inv_s[l, 0], small(l, GAIN))

    def pump_f0(i):
        if i == 0:
            gather_x(0, 0)
            gather_y(1)
            gather_c(0, 0)
            gather_x(0, 1)
            gather_y(2)
        if i == 2:
            gather_c(0, 1)
            gather_x(0, 2)
        if i == 4:
            gather_c(0, 2)
            gather_x(1, 0)

    def pump_f1(i):
        if i == 0:
            gather_c(1, 0)
            gather_x(1, 1)
        if i == 2:
            gather_c(1, 1)
            gather_x(1, 2)
        if i == 4:
            gather_c(1, 2)

    hidden = forward(0, x_ref[s].astype(F32), pump_f0)
    cross_send(0, hidden, 0, out_ref)
    hidden = forward(1, hidden.astype(BF16).astype(F32), pump_f1)
    cross_send_late = hidden

    def pump_b1(i):
        if i == 2:
            reduce_x(1, 2)
        if i == 3:
            reduce_y(1, 2)
            reduce_x(1, 1)

    def pump_b0(i):
        if i == 0:
            reduce_y(1, 1)
            reduce_x(1, 0)
            for g in (1, 2):
                flush(("rc", 1, g))
                flush(("rx", 1, g))
        if i == 2:
            reduce_y(1, 0)
            reduce_x(0, 2)
        if i == 3:
            reduce_y(0, 2)
            reduce_x(0, 1)
            flush(("rc", 1, 0))
            flush(("rx", 1, 0))
        if i == 4:
            reduce_y(0, 1)
            reduce_x(0, 0)

    dy_s[...] = cot_ref[s].astype(F32)
    @pl.when(s == 1)
    def _():
        out_ref[s] = cross_send_late

    @pl.when(s == 0)
    def _():
        xs[0] = cross_send_late

    begin("o", remote(xs.at[0], xr.at[0], o_send.at[0], o_recv.at[0], across), s == 0)

    grad = backward(1, pump_b1).astype(BF16)
    dy_s[...] = grad.astype(F32)
    gm[0, t] = grad
    spread_start(12, gm.at[0])
    cross_send(1, grad.astype(F32), 1, grad_ref)
    grad = backward(0, pump_b0)

    @pl.when(s == 0)
    def _():
        grad_ref[s] = grad

    @pl.when(s == 1)
    def _():
        xs[1] = grad

    begin("o", remote(xs.at[1], xr.at[1], o_send.at[1], o_recv.at[1], across), s == 1)

    a_at = 0
    value = sm[...]
    for buf, me, peers in (
        (arm, c, [mate]), (arx, x, xp), (ary, y, yp), (arz, t, zp)
    ):
        n = len(peers) + 1
        buf[me] = value
        for k in range(1, n):
            begin("a", remote(buf.at[me], buf.at[me], a_send.at[a_at + k], a_recv.at[a_at + k], peers[k - 1]))
        if buf is arm:
            reduce_y(0, 0)
        for k in range(1, n):
            theirs = buf.at[(me - k + n) % n]
            remote(theirs, theirs, a_send.at[a_at + k], a_recv.at[a_at + k], peers[k - 1]).wait_recv()
        value = buf[0]
        for k in range(1, n):
            value = value + buf[k]
        a_at += 4
    small_ref[...] = jnp.where(s == 0, value[:SMALL], value[SMALL:])
    for l in (1, 0):
        for g in (2, 1, 0):
            reduce_done(l, g)
    for index, ref in ((0, out_ref), (1, grad_ref)):
        remote(xs.at[index], xr.at[index], o_send.at[index], o_recv.at[index], across).wait_recv()
        ref[1 - s] = xr[index]
    for key in list(pending):
        flush(key)


def fused(x, cot, seg, shard, gains, offsets, qv, proj, fc):
    vmem = pl.BlockSpec(memory_space=pltpu.VMEM)
    dma = pltpu.SemaphoreType.DMA
    scratch = [
        pltpu.VMEM((2, 8, 2, ROWS, WIDE), BF16),
        pltpu.VMEM((8, 2, ROWS, WIDE), BF16),
        pltpu.VMEM((2, 8, ROWS, WIDE), BF16),
        pltpu.VMEM((2, 3, 2, ROWS, WIDE), BF16),
        pltpu.VMEM((2, 3, ROWS, WIDE), BF16),
        pltpu.VMEM((2, 2, ROWS, WIDE), BF16),
        pltpu.VMEM((2, SMALL, D), F32),
        pltpu.VMEM((2, 4, ROWS, D), BF16),
        pltpu.VMEM((2, 4, ROWS, D), BF16),
        pltpu.VMEM((2, 4, ROWS, D), BF16),
        pltpu.VMEM((2, 4, ROWS, D), BF16),
        pltpu.VMEM((2, 4, ROWS, D), BF16),
        pltpu.VMEM((16, 3, ROWS, D), BF16),
        pltpu.VMEM((2, SEQ, 768), BF16),
        pltpu.VMEM((2, 4, SEQ, SEQ), F32),
        pltpu.VMEM((2, SEQ, 256), BF16),
        pltpu.VMEM((2, SEQ, D), BF16),
        pltpu.VMEM((2, SEQ, D), F32),
        pltpu.VMEM((2, 2, ROWS, D), F32),
        pltpu.VMEM((2, 2, ROWS, 1), F32),
        pltpu.VMEM((ROWS, D), F32),
        pltpu.VMEM((SEQ, D), BF16),
        pltpu.VMEM((SEQ, 768), BF16),
        pltpu.VMEM((D, SEQ), BF16),
        pltpu.VMEM((SEQ, SEQ), F32),
        pltpu.VMEM((ROWS, D), F32),
        pltpu.VMEM((2, ROWS, D), F32),
        pltpu.VMEM((2, ROWS, D), F32),
        pltpu.VMEM((2 * SMALL, D), F32),
        pltpu.VMEM((2, 2 * SMALL, D), F32),
        pltpu.VMEM((4, 2 * SMALL, D), F32),
        pltpu.VMEM((4, 2 * SMALL, D), F32),
        pltpu.VMEM((4, 2 * SMALL, D), F32),
        dma((16, 3)), dma((16, 3)),
        dma((3, 3)), dma((2, 3, 3)),
        dma((2, 3, 3)), dma((2, 3, 3)),
        dma((2, 3)), dma((2, 3)),
        dma((2, 3)), dma((2, 3)),
        dma((2, 3, 3)), dma((2, 3, 3)),
        dma((2, 3, 3)), dma((2, 3, 3)),
        dma((3,)), dma((3,)),
        dma((16,)), dma((16,)),
    ]
    return pl.pallas_call(
        kernel,
        out_shape=(
            jax.ShapeDtypeStruct((2, ROWS, D), F32),
            jax.ShapeDtypeStruct((2, ROWS, D), F32),
            jax.ShapeDtypeStruct((ROWS, WIDE), F32),
            jax.ShapeDtypeStruct((SMALL, D), F32),
        ),
        in_specs=[vmem] * 9,
        out_specs=(vmem,) * 4,
        scratch_shapes=scratch,
        compiler_params=pltpu.CompilerParams(
            collective_id=0, has_side_effects=True, vmem_limit_bytes=62 * 2**20
        ),
    )(x, cot, seg, shard, gains, offsets, qv, proj, fc)


def local(
    inputs, cotangent, segments, qkv_weight, out_weight, fc1_weight, fc2_weight,
    ln_gains, ln_biases, qv_bias, proj_biases, fc_bias,
):
    shard = jnp.concatenate(
        [qkv_weight[0].reshape(ROWS, 768), out_weight[0].T, fc1_weight[0], fc2_weight[0].T], axis=1
    )
    outs, grads, wgrad, small = fused(
        inputs, cotangent, segments, shard, ln_gains[0], ln_biases[0], qv_bias[0], proj_biases[0], fc_bias
    )
    return (
        outs[None],
        grads[None],
        wgrad[:, :768].reshape(1, ROWS, 3, 256),
        wgrad[:, 768:1024].T[None],
        wgrad[:, 1024:2048][None],
        wgrad[:, 2048:].T[None],
        small[GAIN:GAIN + 2][None],
        small[OFFSET:OFFSET + 2][None],
        small[QV:QV + 2][None],
        small[PROJ:PROJ + 2][None],
        small[FC:FC + 4].reshape(1, FF),
    )


def solution(mesh):
    in_specs = (
        P(None, ("dp", "tensor"), None),
        P(None, ("dp", "tensor"), None),
        P(None, "dp", None),
        P("section", "dp", None, "tensor"),
        P("section", "tensor", "dp"),
        P("section", "dp", "tensor"),
        P("section", "tensor", "dp"),
        P("section", None, None),
        P("section", None, None),
        P("section", None, None),
        P("section", None, None),
        P("section", None),
    )
    out_specs = (
        P("section", None, ("dp", "tensor"), None),
        P("section", None, ("dp", "tensor"), None),
        P("section", "dp", None, "tensor"),
        P("section", "tensor", "dp"),
        P("section", "dp", "tensor"),
        P("section", "tensor", "dp"),
        P("section", None, None),
        P("section", None, None),
        P("section", None, None),
        P("section", None, None),
        P("section", None),
    )
    return jax.shard_map(local, mesh=mesh, in_specs=in_specs, out_specs=out_specs, check_vma=False)
```

```python
import functools
import math

import jax
import jax.numpy as jnp
from jax import lax
from jax.experimental import pallas as pl
from jax.experimental.pallas import tpu as pltpu
from jax.sharding import PartitionSpec as P

D = 1024
HD = 64
FF = 4096
SEQ = 256
ROWS = 64
WIDE = 3072
NEGATIVE = -1000000000.0
GELU_COEF = 0.7978845608028654
EPSILON = 1e-05
MESH = pl.DeviceIdType.MESH
BF16 = jnp.bfloat16
F32 = jnp.float32

GAIN, OFFSET, PROJ, QV, FC = 0, 2, 4, 6, 8
SMALL = 16
HALF = ROWS // 2
BOTH = (0, 1)


def scoped(name):
    def deco(func):
        def run(*args, **named):
            with jax.named_scope(name):
                return func(*args, **named)

        return run

    return deco


def dot_nn(a, b):
    return lax.dot_general(a, b, (((1,), (0,)), ((), ())), preferred_element_type=F32)


def dot_nt(a, b):
    return lax.dot_general(a, b, (((1,), (1,)), ((), ())), preferred_element_type=F32)


def dot_tn(a, b):
    return lax.dot_general(a, b, (((0,), (0,)), ((), ())), preferred_element_type=F32)


def norm_rows(hidden, gain_row, offset_row):
    centre = hidden - jnp.mean(hidden, axis=-1, keepdims=True)
    spread = jnp.mean(centre * centre, axis=-1, keepdims=True)
    inverse = lax.rsqrt(spread + EPSILON)
    unit_rows = centre * inverse
    return unit_rows * gain_row + offset_row, unit_rows, inverse


def norm_back(grad_rows, unit_rows, inverse, gain_row):
    grad_unit = grad_rows * gain_row
    return inverse * (
        grad_unit
        - jnp.mean(grad_unit, axis=-1, keepdims=True)
        - unit_rows * jnp.mean(grad_unit * unit_rows, axis=-1, keepdims=True)
    )


def row_sum(value):
    return jnp.sum(value, axis=0, keepdims=True)


def aligned(index, size):
    return pl.ds(pl.multiple_of(index * size, size), size)


def kernel(
    x_ref, cot_ref, seg_ref, qkv_ref, wo_ref, fc1_ref, fc2_ref, gain_ref, offset_ref, qv_ref, proj_ref, fc_ref,
    out_ref, grad_ref, wgrad_ref, late_ref, early_ref,
    w, gd, r0, r1, r2, p1, pb,
    g1, g2, gm, ga, sbuf, rbuf,
    qkv_s, prob_s, mixed_s, active_s, slope_s, unit_s, inv_s, mid_s,
    gb_s, gp_s, gx_s, gt_s, mask_s, dy_s, xs, xr,
    late, early, late_c, late_x, late_y, late_z, early_c, early_x, early_y, early_z,
    z_send, z_recv, gy_send, gy_recv, gx_send, gx_recv, gc_send, gc_recv,
    rc_send, rc_recv, rx_send, rx_recv, ry_send, ry_recv, o_send, o_recv, a_send, a_recv,
):
    s = lax.axis_index("section")
    d = lax.axis_index("dp")
    t = lax.axis_index("tensor")
    x = d // 4
    yl = (d // 2) % 2
    c = d % 2
    y = 2 * s + yl
    mate = {"section": s, "dp": d + 1 - 2 * c, "tensor": t}
    zp = [{"section": s, "dp": d, "tensor": (t + k) % 4} for k in (1, 2, 3)]
    xp = [{"section": s, "dp": ((x + k) % 4) * 4 + yl * 2 + c, "tensor": t} for k in (1, 2, 3)]
    yp = []
    for k in (1, 2, 3):
        other = (y + k) % 4
        yp.append({"section": other // 2, "dp": x * 4 + (other % 2) * 2 + c, "tensor": t})
    across = {"section": 1 - s, "dp": d, "tensor": t}

    def remote(src, dst, send, recv, peer):
        return pltpu.make_async_remote_copy(
            src_ref=src, dst_ref=dst, send_sem=send, recv_sem=recv, device_id=peer, device_id_type=MESH
        )

    pending = {}

    def begin(key, copy, cond=None):
        if cond is None:
            copy.start()
        else:
            pl.when(cond)(copy.start)
        pending.setdefault(key, []).append((copy, cond))

    def flush(key):
        for copy, cond in pending.pop(key, []):
            if cond is None:
                copy.wait_send()
            else:
                pl.when(cond)(copy.wait_send)

    barrier = pltpu.get_barrier_semaphore()
    for peer in zp + xp + yp + [mate]:
        pl.semaphore_signal(barrier, inc=1, device_id=peer, device_id_type=MESH)
    pl.semaphore_wait(barrier, 10)

    def cols(g):
        return pl.ds(g * 1024, 1024)

    def own(g):
        return w.at[s, x, yl, c, :, cols(g)]

    def rows(h):
        return slice(h * HALF, (h + 1) * HALF)

    def part(h):
        return pl.ds(h * HALF, HALF)

    def gather_y(g):
        for k in (1, 2, 3):
            begin("gy", remote(
                own(g), own(g),
                gy_send.at[g, k - 1], gy_recv.at[s, g, k - 1], yp[k - 1],
            ))

    @scoped("gather_x")
    def gather_x(l, g):
        for k in (1, 2, 3):
            src_y = (y - k + 4) % 4
            copy = remote(
                own(g), w.at[l, x, src_y % 2, c, :, cols(g)],
                gy_send.at[g, k - 1], gy_recv.at[l, g, k - 1], yp[k - 1],
            )
            pl.when(src_y // 2 == l)(copy.wait_recv)
        mine = w.at[l, x, :, c, :, cols(g)]
        for k in (1, 2, 3):
            begin("gx", remote(mine, mine, gx_send.at[l, g, k - 1], gx_recv.at[l, g, k - 1], xp[k - 1]))

    @scoped("gather_c")
    def gather_c(l, g):
        for k in (1, 2, 3):
            theirs = w.at[l, (x - k + 4) % 4, :, c, :, cols(g)]
            remote(theirs, theirs, gx_send.at[l, g, k - 1], gx_recv.at[l, g, k - 1], xp[k - 1]).wait_recv()
        half = w.at[l, :, :, c, :, cols(g)]
        begin("gc", remote(half, half, gc_send.at[l, g], gc_recv.at[l, g], mate))

    def turn_x(g):
        for k in (1, 2, 3):
            begin("gx", remote(
                own(g), own(g),
                gx_send.at[0, g, k - 1], gx_recv.at[0, g, k - 1], xp[k - 1],
            ))

    @scoped("turn_y")
    def turn_y(g):
        for k in (1, 2, 3):
            remote(
                own(g), w.at[s, (x - k + 4) % 4, yl, c, :, cols(g)],
                gx_send.at[0, g, k - 1], gx_recv.at[0, g, k - 1], xp[k - 1],
            ).wait_recv()
        mine = w.at[s, :, yl, c, :, cols(g)]
        for k in (1, 2, 3):
            begin("gy", remote(mine, mine, gy_send.at[g, k - 1], gy_recv.at[s, g, k - 1], yp[k - 1]))

    @scoped("turn_c")
    def turn_c(l, g):
        for k in (1, 2, 3):
            src_y = (y - k + 4) % 4
            theirs = w.at[l, :, src_y % 2, c, :, cols(g)]
            copy = remote(theirs, theirs, gy_send.at[g, k - 1], gy_recv.at[l, g, k - 1], yp[k - 1])
            pl.when(src_y // 2 == l)(copy.wait_recv)
        half = w.at[l, :, :, c, :, cols(g)]
        begin("gc", remote(half, half, gc_send.at[l, g], gc_recv.at[l, g], mate))

    @scoped("gather_done")
    def gather_done(l, g):
        half = w.at[l, :, :, 1 - c, :, cols(g)]
        remote(half, half, gc_send.at[l, g], gc_recv.at[l, g], mate).wait_recv()

    def reduce_c(l, g):
        begin(("rc", l, g), remote(
            gd.at[:, :, 1 - c, :, cols(g)], r0.at[l, :, :, :, cols(g)], rc_send.at[l, g], rc_recv.at[l, g], mate
        ))

    @scoped("reduce_x")
    def reduce_x(l, g):
        remote(
            gd.at[:, :, 1 - c, :, cols(g)], r0.at[l, :, :, :, cols(g)], rc_send.at[l, g], rc_recv.at[l, g], mate
        ).wait_recv()

        def add(i, _):
            for half in BOTH:
                gd[i, half, c, :, cols(g)] = (
                    gd[i, half, c, :, cols(g)].astype(F32) + r0[l, i, half, :, cols(g)].astype(F32)
                ).astype(BF16)
            return 0

        lax.fori_loop(0, 4, add, 0)
        for i in range(4):
            begin(("rx", l, g), x_copy(l, g, i))

    def x_copy(l, g, i):
        step, half = ((2, 0), (2, 1), (1, 1), (3, 0), (1, 0), (3, 1))[i]
        return remote(
            gd.at[(x + step) % 4, half, c, :, cols(g)], r1.at[l, i, :, cols(g)],
            rx_send.at[l, g, i], rx_recv.at[l, g, i], xp[2 * (i % 2)],
        )

    @scoped("reduce_f")
    def reduce_f(l, g):
        for i in BOTH:
            x_copy(l, g, i).wait_recv()
            at = (x + 1 + 2 * i) % 4
            gd[at, i, c, :, cols(g)] = (
                gd[at, i, c, :, cols(g)].astype(F32) + r1[l, i, :, cols(g)].astype(F32)
            ).astype(BF16)
            begin(("rx", l, g), x_copy(l, g, 4 + i))

    @scoped("reduce_y")
    def reduce_y(l, g):
        for i in (2, 3, 4, 5):
            x_copy(l, g, i).wait_recv()
        for half in BOTH:
            total = gd[x, half, c, :, cols(g)].astype(F32)
            for i in ((3, 4), (2, 5))[half]:
                total += r1[l, i, :, cols(g)].astype(F32)
            p1[l, half, :, cols(g)] = total.astype(BF16)
        for k in (1, 2, 3):
            target = (y + k) % 4
            begin("ry", remote(
                p1.at[l, target % 2, :, cols(g)], r2.at[l, k - 1, :, cols(g)],
                ry_send.at[l, g, k - 1], ry_recv.at[l, g, k - 1], yp[k - 1],
            ), target // 2 == l)

    @scoped("reduce_done")
    def reduce_done(l, g):
        copies = [
            remote(
                p1.at[l, 0, :, cols(g)], r2.at[l, k, :, cols(g)],
                ry_send.at[l, g, k], ry_recv.at[l, g, k], yp[k],
            )
            for k in (0, 1, 2)
        ]

        @pl.when(s == l)
        def _():
            for copy in copies:
                copy.wait_recv()
            total = p1[l, yl, :, cols(g)].astype(F32)
            for k in (0, 1, 2):
                total += r2[l, k, :, cols(g)].astype(F32)
            wgrad_ref[:, cols(g)] = total

    def spread_start(event, buf, h):
        mine = buf.at[t, part(h)]
        for k in (1, 2, 3):
            begin("z", remote(mine, mine, z_send.at[event, h, k - 1], z_recv.at[event, h, k - 1], zp[k - 1]))

    @scoped("spread_done")
    def spread_done(event, buf, h):
        for k in (1, 2, 3):
            theirs = buf.at[(t - k + 4) % 4, part(h)]
            remote(theirs, theirs, z_send.at[event, h, k - 1], z_recv.at[event, h, k - 1], zp[k - 1]).wait_recv()

    def sum_copy(event, h, k):
        return remote(
            sbuf.at[(event // 2) % 3, (t + k) % 4, part(h)], rbuf.at[event // 2, k - 1, part(h)],
            z_send.at[event, h, k - 1], z_recv.at[event, h, k - 1], zp[k - 1],
        )

    def sum_start(event, h):
        for k in (1, 2, 3):
            begin(("s", (event // 2) % 3, h), sum_copy(event, h, k))

    @scoped("sum_done")
    def sum_done(event, h):
        for k in (1, 2, 3):
            sum_copy(event, h, k).wait_recv()
        total = sbuf[(event // 2) % 3, t, rows(h)].astype(F32)
        for k in (0, 1, 2):
            total += rbuf[event // 2, k, rows(h)].astype(F32)
        return total

    @scoped("share")
    def share(event, h, lhs, l, c0, n):
        slot = (event // 2) % 3
        flush(("s", slot, h))

        def tile(j, _):
            right = w[l, j, :, :, :, pl.ds(c0, n)].reshape(256, n)
            value = dot_nt(lhs().reshape(4 * HALF, n), right).astype(BF16)
            sbuf[slot, :, rows(h), aligned(j, 256)] = value.reshape(4, HALF, 256)
            return 0

        lax.fori_loop(0, 4, tile, 0)
        sum_start(event, h)

    fills = []

    def fill(count):
        for _ in range(min(count, len(fills))):
            fills.pop(0)()

    def weight_grad(lhs_ref, rhs_ref, c0, n, then=None):
        @scoped("weight_grad")
        def one(i):
            left = lhs_ref[:, :, i * 256:(i + 1) * 256].reshape(SEQ, 256).T
            gt_s[...] = left

            def tile(j, _):
                value = dot_nn(gt_s[...], rhs_ref[:, :, aligned(j, 256)].reshape(SEQ, 256))
                gd[i, :, :, :, pl.ds(pl.multiple_of(c0 + j * 256, 256), 256)] = value.astype(
                    BF16
                ).reshape(2, 2, ROWS, 256)
                return 0

            lax.fori_loop(0, n // 256, tile, 0)
            if then is not None and i == 3:
                then()

        for i in range(4):
            fills.append(functools.partial(one, i))

    def cross_send(index, value, l, local_ref, h):
        @pl.when(s == l)
        def _():
            local_ref[s, rows(h)] = value

        @pl.when(s != l)
        def _():
            xs[index, rows(h)] = value

        begin("o", remote(
            xs.at[index, part(h)], xr.at[index, part(h)], o_send.at[index, h], o_recv.at[index, h], across
        ), s != l)

    stages = {
        "c": ((late_c, early_c), c, [mate], 0), "x": ((late_x, early_x), x, xp, 1),
        "y": ((late_y, early_y), y, yp, 4), "z": ((late_z, early_z), t, zp, 7),
    }

    def all_sum(kind, l, stage):
        bufs, _, peers, _ = stages[stage]
        value = bufs[kind][l, 0]
        for k in range(1, len(peers) + 1):
            value = value + bufs[kind][l, k]
        return value

    def all_start(kind, l, stage, before=None):
        bufs, me, peers, at = stages[stage]
        buf = bufs[kind]
        buf[l, me] = (late, early)[kind][l] if before is None else all_sum(kind, l, before)
        for k, peer in enumerate(peers):
            begin("a", remote(
                buf.at[l, me], buf.at[l, me], a_send.at[kind, l, at + k], a_recv.at[kind, l, at + k], peer
            ))

    @scoped("all_wait")
    def all_wait(kind, l, stage):
        bufs, me, peers, at = stages[stage]
        n = len(peers) + 1
        for k, peer in enumerate(peers):
            theirs = bufs[kind].at[l, (me - k - 1 + n) % n]
            remote(theirs, theirs, a_send.at[kind, l, at + k], a_recv.at[kind, l, at + k], peer).wait_recv()

    def all_next(kind, l, stage, following):
        all_wait(kind, l, stage)
        all_start(kind, l, following, stage)

    def small(l, row):
        return pb[l, row:row + 1]

    def norm_one(l, h, hidden):
        normed, unit, inverse = norm_rows(hidden, small(l, GAIN), small(l, OFFSET))
        unit_s[l, 0, rows(h)] = unit
        inv_s[l, 0, rows(h)] = inverse
        g1[l, t, rows(h)] = normed.astype(BF16)
        spread_start(4 * l, g1.at[l], h)
        mid_s[rows(h)] = hidden

    def project(l, h):
        left = g1[l, :, rows(h)].reshape(4 * HALF, D)
        for j in range(3):
            value = dot_nn(left, w[l, :, :, :, :, j * 256:(j + 1) * 256].reshape(D, 256))
            if j != 1:
                value = value + pb[l, QV + j // 2:QV + j // 2 + 1, aligned(t, 256)]
            qkv_s[l, :, rows(h), j * 256:(j + 1) * 256] = value.astype(BF16).reshape(4, HALF, 256)

    def head(l, j, n):
        return qkv_s[l, :, :, j * 256 + n * HD:j * 256 + (n + 1) * HD].reshape(SEQ, HD)

    @scoped("attend")
    def attend(l):
        for pair in range(2):
            mixed = []
            for n in (2 * pair, 2 * pair + 1):
                scores = dot_nt(head(l, 0, n), head(l, 1, n)) * 0.125
                scores = jnp.where(mask_s[...] > 0.5, scores, NEGATIVE)
                shifted = jnp.exp(scores - jnp.max(scores, axis=-1, keepdims=True))
                probs = shifted / jnp.sum(shifted, axis=-1, keepdims=True)
                prob_s[l, n] = probs
                mixed.append(dot_nn(probs.astype(BF16), head(l, 2, n)))
            both = jnp.concatenate(mixed, axis=1).astype(BF16)
            mixed_s[l, :, :, pair * 128:(pair + 1) * 128] = both.reshape(4, ROWS, 128)

    def norm_two(l, h):
        middle = mid_s[rows(h)] + (sum_done(4 * l + 1, h) + small(l, PROJ))
        normed, unit, inverse = norm_rows(middle, small(l, GAIN + 1), small(l, OFFSET + 1))
        unit_s[l, 1, rows(h)] = unit
        inv_s[l, 1, rows(h)] = inverse
        g2[l, t, rows(h)] = normed.astype(BF16)
        spread_start(4 * l + 2, g2.at[l], h)
        mid_s[rows(h)] = middle

    @scoped("up")
    def up(l, h):
        def tile(j, _):
            at = aligned(j, 256)
            before = dot_nn(
                g2[l, :, rows(h)].reshape(4 * HALF, D),
                w[l, :, :, :, :, pl.ds(pl.multiple_of(1024 + j * 256, 256), 256)].reshape(D, 256),
            ) + pb[l, pl.ds(FC + t, 1), at]
            tanh_part = jnp.tanh(GELU_COEF * (before + 0.044715 * before * before * before))
            active = (0.5 * before * (1.0 + tanh_part)).astype(BF16)
            slope = 0.5 * (1.0 + tanh_part) + 0.5 * before * (
                1.0 - tanh_part * tanh_part
            ) * GELU_COEF * (1.0 + 3.0 * 0.044715 * before * before)
            active_s[l, :, rows(h), at] = active.reshape(4, HALF, 256)
            if l == 0:
                slope_s[l, :, rows(h), at] = slope.reshape(4, HALF, 256)
            else:
                grad_before = slope_s[l, :, rows(h), at].reshape(4 * HALF, 256) * slope
                early[l, pl.ds(4 + t, 1), at] += row_sum(grad_before)
                gb_s[:, rows(h), at] = grad_before.astype(BF16).reshape(4, HALF, 256)
            return 0

        lax.fori_loop(0, 4, tile, 0)

    def layer_out(l, h):
        return mid_s[rows(h)] + (sum_done(4 * l + 3, h) + small(l, PROJ + 1))

    def attention_part(l):
        for h in BOTH:
            spread_done(4 * l, g1.at[l], h)
            if h == 0:
                gather_done(l, 0)
            project(l, h)
        attend(l)
        for h in BOTH:
            share(4 * l + 1, h, lambda h=h: mixed_s[l, :, rows(h)], l, 768, 256)

    @scoped("before_up")
    def before_up(l):
        def tile(j, _):
            value = dot_nn(
                gm[l].reshape(SEQ, D),
                w[l, :, :, :, :, pl.ds(pl.multiple_of(2048 + j * 256, 256), 256)].reshape(D, 256),
            )
            slope_s[l, :, :, aligned(j, 256)] = value.reshape(4, ROWS, 256)
            return 0

        lax.fori_loop(0, 4, tile, 0)

    @scoped("down")
    def down(l, h):
        def tile(j, _):
            at = aligned(j, 256)
            grad_before = dot_nn(
                gm[l, :, rows(h)].reshape(4 * HALF, D),
                w[l, :, :, :, :, pl.ds(pl.multiple_of(2048 + j * 256, 256), 256)].reshape(D, 256),
            ) * slope_s[l, :, rows(h), at].reshape(4 * HALF, 256)
            early[l, pl.ds(4 + t, 1), at] += row_sum(grad_before)
            gb_s[:, rows(h), at] = grad_before.astype(BF16).reshape(4, HALF, 256)
            return 0

        lax.fori_loop(0, 4, tile, 0)

    def norm_two_back(l, h):
        grad = sum_done(13 - 4 * l, h)
        unit = unit_s[l, 1, rows(h)]
        early[l, 0:1] += row_sum(grad * unit)
        early[l, 1:2] += row_sum(grad)
        grad_middle = dy_s[rows(h)] + norm_back(grad, unit, inv_s[l, 1, rows(h)], small(l, GAIN + 1))
        dy_s[rows(h)] = grad_middle
        ga[l, t, rows(h)] = grad_middle.astype(BF16)
        spread_start(14 - 4 * l, ga.at[l], h)
        early[l, 2:3] += row_sum(grad_middle)

    def mixed_back(l, h):
        value = dot_nn(
            ga[l, :, rows(h)].reshape(4 * HALF, D), w[l, :, :, :, :, 768:1024].reshape(D, 256)
        )
        gx_s[:, rows(h)] = value.astype(BF16).reshape(4, HALF, 256)

    @scoped("attend_back")
    def attend_back(l):
        for pair in range(2):
            grads = [[], [], []]
            for n in (2 * pair, 2 * pair + 1):
                q, key, value = head(l, 0, n), head(l, 1, n), head(l, 2, n)
                grad_head = gx_s[:, :, n * HD:(n + 1) * HD].reshape(SEQ, HD)
                probs = prob_s[l, n]
                grad_probs = dot_nt(grad_head, value)
                row_dot = jnp.sum(probs * grad_probs, axis=-1, keepdims=True)
                grad_scores = (probs * (grad_probs - row_dot)).astype(BF16)
                grads[0].append(dot_nn(grad_scores, key) * 0.125)
                grads[1].append(dot_tn(grad_scores, q) * 0.125)
                grads[2].append(dot_tn(probs.astype(BF16), grad_head))
            for j in range(3):
                both = jnp.concatenate(grads[j], axis=1)
                gp_s[:, :, j * 256 + pair * 128:j * 256 + (pair + 1) * 128] = both.astype(BF16).reshape(
                    4, ROWS, 128
                )
                if j != 1:
                    total = row_sum(both)
                    for k in BOTH:
                        late[l, 4 + j + k:5 + j + k, aligned((t % 2) * 2 + pair, 128)] = jnp.where(
                            t // 2 == k, total, 0.0
                        )

    def norm_one_back(l, h):
        grad = sum_done(15 - 4 * l, h)
        unit = unit_s[l, 0, rows(h)]
        for row, value in ((0, row_sum(grad * unit)), (2, row_sum(grad))):
            late[l, row:row + 1] += value[:, :512]
            late[l, row + 1:row + 2] += value[:, 512:]
        return dy_s[rows(h)] + norm_back(grad, unit, inv_s[l, 0, rows(h)], small(l, GAIN))

    pb[s, GAIN:GAIN + 2] = gain_ref[...]
    pb[s, OFFSET:OFFSET + 2] = offset_ref[...]
    pb[s, PROJ:PROJ + 2] = proj_ref[...]
    pb[s, QV:QV + 2] = qv_ref[...]
    for k in range(4):
        pb[s, FC + k:FC + k + 1] = fc_ref[:, k * 1024:(k + 1) * 1024]
    pb[s, FC + 4:] = jnp.zeros((SMALL - FC - 4, D), F32)
    begin("pb", remote(pb.at[s], pb.at[s], o_send.at[2, 0], o_recv.at[2, 0], across))
    for j in range(3):
        w[s, x, yl, c, :, j * 256:(j + 1) * 256] = qkv_ref[j]
    w[s, x, yl, c, :, 768:1024] = wo_ref[...]
    gather_y(0)
    w[s, x, yl, c, :, 2048:] = fc2_ref[...]
    turn_x(2)
    w[s, x, yl, c, :, 1024:2048] = fc1_ref[...]
    late[...] = jnp.zeros_like(late)
    early[...] = jnp.zeros_like(early)
    seg_rows = jnp.broadcast_to(seg_ref[s].astype(F32), (SEQ, SEQ))
    seg_cols = seg_rows.T
    places_i = lax.broadcasted_iota(jnp.int32, (SEQ, SEQ), 0)
    places_j = lax.broadcasted_iota(jnp.int32, (SEQ, SEQ), 1)
    mask_s[...] = jnp.where((seg_rows == seg_cols) & (places_i >= places_j), 1.0, 0.0)
    with jax.named_scope("wait_pb"):
        remote(pb.at[1 - s], pb.at[1 - s], o_send.at[2, 0], o_recv.at[2, 0], across).wait_recv()
    for h in BOTH:
        norm_one(0, h, x_ref[s, rows(h)].astype(F32))
    gather_x(0, 0)
    gather_y(1)
    turn_y(2)
    gm[1, t] = cot_ref[s]
    for h in BOTH:
        spread_start(8, gm.at[1], h)
    dy_s[...] = cot_ref[s].astype(F32)
    early[1, 3:4] = row_sum(dy_s[...])
    gather_c(0, 0)
    gather_x(0, 1)

    attention_part(0)
    for h in BOTH:
        norm_two(0, h)
    gather_c(0, 1)
    gather_x(1, 0)
    for h in BOTH:
        spread_done(2, g2.at[0], h)
        if h == 0:
            gather_done(0, 1)
        up(0, h)
        if h == 0:
            turn_c(0, 2)
            gather_done(0, 2)
        share(3, h, lambda h=h: active_s[0, :, rows(h)], 0, 2048, 1024)
    turn_c(1, 2)
    gather_c(1, 0)
    gather_x(1, 1)
    for h in BOTH:
        hidden = layer_out(0, h)
        norm_one(1, h, hidden.astype(BF16).astype(F32))
        cross_send(0, hidden, 0, out_ref, h)

    attention_part(1)
    gather_done(1, 2)
    for h in BOTH:
        spread_done(8, gm.at[1], h)
    before_up(1)
    for h in BOTH:
        norm_two(1, h)
    gather_c(1, 1)
    weight_grad(gm.at[1], active_s.at[1], 2048, 1024, lambda: reduce_c(1, 2))
    weight_grad(g2.at[1], gb_s, 1024, 1024, lambda: reduce_c(1, 1))
    for h in BOTH:
        spread_done(6, g2.at[1], h)
        if h == 0:
            gather_done(1, 1)
        up(1, h)
        share(9, h, lambda h=h: gb_s[:, rows(h)], 1, 1024, 1024)
    fill(4)
    norm_two_back(1, 0)
    fill(2)
    norm_two_back(1, 1)
    fill(1)
    reduce_x(1, 2)
    fill(1)
    share(7, 0, lambda: active_s[1, :, rows(0)], 1, 2048, 1024)
    spread_done(10, ga.at[1], 0)
    mixed_back(1, 0)
    share(7, 1, lambda: active_s[1, :, rows(1)], 1, 2048, 1024)
    spread_done(10, ga.at[1], 1)
    mixed_back(1, 1)
    reduce_x(1, 1)
    attend_back(1)
    for h in BOTH:
        share(11, h, lambda h=h: gp_s[:, rows(h)], 1, 0, 768)
    reduce_f(1, 2)
    weight_grad(ga.at[1], mixed_s.at[1], 768, 256)
    weight_grad(g1.at[1], gp_s, 0, 768, lambda: reduce_c(1, 0))
    fill(8)

    def pass_grad(h):
        grad = norm_one_back(1, h).astype(BF16)
        gm[0, t, rows(h)] = grad
        spread_start(12, gm.at[0], h)
        dy_s[rows(h)] = grad.astype(F32)
        cross_send(3, grad.astype(F32), 1, grad_ref, h)

    pass_grad(0)
    reduce_f(1, 1)
    for h in BOTH:
        hidden = layer_out(1, h)
        cross_send(2, hidden, 1, out_ref, h)
    pass_grad(1)
    reduce_x(1, 0)
    reduce_y(1, 2)
    early[0, 3:4] = row_sum(dy_s[...])
    for kind in BOTH:
        all_start(kind, 1, "c")
    flush(("rc", 1, 2))
    flush(("rx", 1, 2))

    for h in BOTH:
        spread_done(12, gm.at[0], h)
        down(0, h)
        share(13, h, lambda h=h: gb_s[:, rows(h)], 0, 1024, 1024)
    reduce_f(1, 0)
    weight_grad(gm.at[0], active_s.at[0], 2048, 1024, lambda: reduce_c(0, 2))
    weight_grad(g2.at[0], gb_s, 1024, 1024, lambda: reduce_c(0, 1))
    fill(4)
    norm_two_back(0, 0)
    reduce_y(1, 1)
    flush(("rc", 1, 1))
    flush(("rx", 1, 1))
    fill(2)
    norm_two_back(0, 1)
    reduce_x(0, 2)
    fill(2)
    for kind in BOTH:
        all_next(kind, 1, "c", "y")
    spread_done(14, ga.at[0], 0)
    mixed_back(0, 0)
    reduce_y(1, 0)
    flush(("rc", 1, 0))
    flush(("rx", 1, 0))
    spread_done(14, ga.at[0], 1)
    mixed_back(0, 1)
    reduce_x(0, 1)
    attend_back(0)
    for h in BOTH:
        share(15, h, lambda h=h: gp_s[:, rows(h)], 0, 0, 768)
    reduce_f(0, 2)
    all_start(1, 0, "c")
    weight_grad(ga.at[0], mixed_s.at[0], 768, 256)
    weight_grad(g1.at[0], gp_s, 0, 768, lambda: reduce_c(0, 0))
    fill(8)
    cross_send(1, norm_one_back(0, 0), 0, grad_ref, 0)
    reduce_f(0, 1)
    all_next(1, 0, "c", "y")
    for kind in BOTH:
        all_next(kind, 1, "y", "x")
    cross_send(1, norm_one_back(0, 1), 0, grad_ref, 1)
    all_start(0, 0, "c")
    reduce_x(0, 0)
    all_next(0, 0, "c", "z")
    reduce_y(0, 2)
    for kind in BOTH:
        all_next(kind, 1, "x", "z")
    all_next(1, 0, "y", "x")
    reduce_y(0, 1)
    all_next(0, 0, "z", "y")
    reduce_f(0, 0)
    all_next(0, 0, "y", "x")
    all_next(1, 0, "x", "z")
    for g in (2, 1, 0):
        reduce_done(1, g)
    for kind in BOTH:
        all_wait(kind, 1, "z")
    reduce_y(0, 0)
    all_wait(0, 0, "x")
    all_wait(1, 0, "z")
    for kind, ref in ((0, late_ref), (1, early_ref)):
        ref[...] = jnp.where(s == 0, all_sum(kind, 0, "zx"[1 - kind]), all_sum(kind, 1, "z"))
    for ref, pairs in ((out_ref, (0, 2)), (grad_ref, (1, 3))):
        for h in BOTH:
            first, second = [
                remote(
                    xs.at[index, part(h)], xr.at[index, part(h)], o_send.at[index, h], o_recv.at[index, h], across
                )
                for index in pairs
            ]
            pl.when(s == 0)(first.wait_recv)
            pl.when(s == 1)(second.wait_recv)

        @pl.when(s == 0)
        def _():
            ref[1 - s] = xr[pairs[0]]

        @pl.when(s == 1)
        def _():
            ref[1 - s] = xr[pairs[1]]

    for g in (2, 1, 0):
        reduce_done(0, g)
    for key in list(pending):
        flush(key)


def finish(
    out_ref, grad_ref, wgrad_ref, late_ref, early_ref,
    outs, grads, qkv, out, fc1, fc2, gain, offset, qv, proj, fc,
):
    outs[0] = out_ref[...]
    grads[0] = grad_ref[...]
    for j in range(3):
        qkv[0, j] = wgrad_ref[:, j * 256:(j + 1) * 256]
    out[0] = wgrad_ref[:, 768:1024]
    fc1[0] = wgrad_ref[:, 1024:2048]
    fc2[0] = wgrad_ref[:, 2048:]
    for ref, row, other in ((gain, 0, 0), (offset, 2, 1)):
        for k in BOTH:
            ref[0, 0:1, k * 512:(k + 1) * 512] = late_ref[row + k:row + k + 1]
        ref[0, 1:2] = early_ref[other:other + 1]
    for row in BOTH:
        for k in BOTH:
            at = 4 + 2 * row + k
            qv[0, row:row + 1, k * 512:(k + 1) * 512] = late_ref[at:at + 1]
    proj[0] = early_ref[2:4]
    for k in range(4):
        fc[:, k * 1024:(k + 1) * 1024] = early_ref[4 + k:5 + k]


def fused(*args):
    vmem = pl.BlockSpec(memory_space=pltpu.VMEM)
    dma = pltpu.SemaphoreType.DMA
    scratch = [
        pltpu.VMEM((2, 4, 2, 2, ROWS, WIDE), BF16),
        pltpu.VMEM((4, 2, 2, ROWS, WIDE), BF16),
        pltpu.VMEM((2, 4, 2, ROWS, WIDE), BF16),
        pltpu.VMEM((2, 6, ROWS, WIDE), BF16),
        pltpu.VMEM((2, 3, ROWS, WIDE), BF16),
        pltpu.VMEM((2, 2, ROWS, WIDE), BF16),
        pltpu.VMEM((2, SMALL, D), F32),
        pltpu.VMEM((2, 4, ROWS, D), BF16),
        pltpu.VMEM((2, 4, ROWS, D), BF16),
        pltpu.VMEM((2, 4, ROWS, D), BF16),
        pltpu.VMEM((2, 4, ROWS, D), BF16),
        pltpu.VMEM((3, 4, ROWS, D), BF16),
        pltpu.VMEM((8, 3, ROWS, D), BF16),
        pltpu.VMEM((2, 4, ROWS, 768), BF16),
        pltpu.VMEM((2, 4, SEQ, SEQ), F32),
        pltpu.VMEM((2, 4, ROWS, 256), BF16),
        pltpu.VMEM((2, 4, ROWS, D), BF16),
        pltpu.VMEM((2, 4, ROWS, D), F32),
        pltpu.VMEM((2, 2, ROWS, D), F32),
        pltpu.VMEM((2, 2, ROWS, 1), F32),
        pltpu.VMEM((ROWS, D), F32),
        pltpu.VMEM((4, ROWS, D), BF16),
        pltpu.VMEM((4, ROWS, 768), BF16),
        pltpu.VMEM((4, ROWS, 256), BF16),
        pltpu.VMEM((256, SEQ), BF16),
        pltpu.VMEM((SEQ, SEQ), F32),
        pltpu.VMEM((ROWS, D), F32),
        pltpu.VMEM((4, ROWS, D), F32),
        pltpu.VMEM((4, ROWS, D), F32),
        pltpu.VMEM((2, 8, 512), F32),
        pltpu.VMEM((2, 8, D), F32),
    ]
    for width in (512, D):
        scratch += [pltpu.VMEM((2, n, 8, width), F32) for n in (2, 4, 4, 4)]
    scratch += [
        dma((16, 2, 3)), dma((16, 2, 3)),
        dma((3, 3)), dma((2, 3, 3)),
        dma((2, 3, 3)), dma((2, 3, 3)),
        dma((2, 3)), dma((2, 3)),
        dma((2, 3)), dma((2, 3)),
        dma((2, 3, 6)), dma((2, 3, 6)),
        dma((2, 3, 3)), dma((2, 3, 3)),
        dma((4, 2)), dma((4, 2)),
        dma((2, 2, 10)), dma((2, 2, 10)),
    ]
    sums = pl.pallas_call(
        kernel,
        out_shape=(
            jax.ShapeDtypeStruct((2, ROWS, D), F32),
            jax.ShapeDtypeStruct((2, ROWS, D), F32),
            jax.ShapeDtypeStruct((ROWS, WIDE), F32),
            jax.ShapeDtypeStruct((8, 512), F32),
            jax.ShapeDtypeStruct((8, D), F32),
        ),
        in_specs=[vmem] * 12,
        out_specs=(vmem,) * 5,
        scratch_shapes=scratch,
        compiler_params=pltpu.CompilerParams(
            collective_id=0, has_side_effects=True, vmem_limit_bytes=62 * 2**20
        ),
    )(*args)
    return pl.pallas_call(
        finish,
        out_shape=(
            jax.ShapeDtypeStruct((1, 2, ROWS, D), F32),
            jax.ShapeDtypeStruct((1, 2, ROWS, D), F32),
            jax.ShapeDtypeStruct((1, 3, ROWS, 256), F32),
            jax.ShapeDtypeStruct((1, ROWS, 256), F32),
            jax.ShapeDtypeStruct((1, ROWS, 1024), F32),
            jax.ShapeDtypeStruct((1, ROWS, 1024), F32),
            jax.ShapeDtypeStruct((1, 2, D), F32),
            jax.ShapeDtypeStruct((1, 2, D), F32),
            jax.ShapeDtypeStruct((1, 2, D), F32),
            jax.ShapeDtypeStruct((1, 2, D), F32),
            jax.ShapeDtypeStruct((1, FF), F32),
        ),
        in_specs=[vmem] * 5,
        out_specs=(vmem,) * 11,
    )(*sums)


def local(
    inputs, cotangent, segments, qkv_weight, out_weight, fc1_weight, fc2_weight,
    ln_gains, ln_biases, qv_bias, proj_biases, fc_bias,
):
    outs, grads, qkv, out, fc1, fc2, gain, offset, qv, proj, fc = fused(
        inputs, cotangent, segments,
        jnp.transpose(qkv_weight[0], (1, 0, 2)), out_weight[0].T, fc1_weight[0], fc2_weight[0].T,
        ln_gains[0], ln_biases[0], qv_bias[0], proj_biases[0], fc_bias,
    )
    return (
        outs, grads, jnp.transpose(qkv, (0, 2, 1, 3)), jnp.transpose(out, (0, 2, 1)), fc1,
        jnp.transpose(fc2, (0, 2, 1)), gain, offset, qv, proj, fc,
    )


def solution(mesh):
    in_specs = (
        P(None, ("dp", "tensor"), None),
        P(None, ("dp", "tensor"), None),
        P(None, "dp", None),
        P("section", "dp", None, "tensor"),
        P("section", "tensor", "dp"),
        P("section", "dp", "tensor"),
        P("section", "tensor", "dp"),
        P("section", None, None),
        P("section", None, None),
        P("section", None, None),
        P("section", None, None),
        P("section", None),
    )
    out_specs = (
        P("section", None, ("dp", "tensor"), None),
        P("section", None, ("dp", "tensor"), None),
        P("section", "dp", None, "tensor"),
        P("section", "tensor", "dp"),
        P("section", "dp", "tensor"),
        P("section", "tensor", "dp"),
        P("section", None, None),
        P("section", None, None),
        P("section", None, None),
        P("section", None, None),
        P("section", None),
    )
    return jax.shard_map(local, mesh=mesh, in_specs=in_specs, out_specs=out_specs, check_vma=False)
```

```python
import functools
import math

import jax
import jax.numpy as jnp
from jax import lax
from jax.experimental import pallas as pl
from jax.experimental.pallas import tpu as pltpu
from jax.sharding import PartitionSpec as P

D = 1024
HD = 64
FF = 4096
SEQ = 256
ROWS = 64
WIDE = 3072
NEGATIVE = -1000000000.0
GELU_COEF = 0.7978845608028654
EPSILON = 1e-05
MESH = pl.DeviceIdType.MESH
BF16 = jnp.bfloat16
F32 = jnp.float32

GAIN, OFFSET, PROJ, QV, FC = 0, 2, 4, 6, 8
SMALL = 16
HALF = ROWS // 2
BOTH = (0, 1)
GATHER = ((0, 768), (768, 256), (1024, 512), (1536, 512), (2048, 256), (2304, 768))
REDUCE = ((0, 768), (768, 256), (1024, 1024), (2048, 512), (2560, 512))


def scoped(name):
    def deco(func):
        def run(*args, **named):
            with jax.named_scope(name):
                return func(*args, **named)

        return run

    return deco


def dot_nn(a, b):
    return lax.dot_general(a, b, (((1,), (0,)), ((), ())), preferred_element_type=F32)


def dot_nt(a, b):
    return lax.dot_general(a, b, (((1,), (1,)), ((), ())), preferred_element_type=F32)


def dot_tn(a, b):
    return lax.dot_general(a, b, (((0,), (0,)), ((), ())), preferred_element_type=F32)


def norm_rows(hidden, gain_row, offset_row):
    centre = hidden - jnp.mean(hidden, axis=-1, keepdims=True)
    spread = jnp.mean(centre * centre, axis=-1, keepdims=True)
    inverse = lax.rsqrt(spread + EPSILON)
    unit_rows = centre * inverse
    return unit_rows * gain_row + offset_row, unit_rows, inverse


def norm_back(grad_rows, unit_rows, inverse, gain_row):
    grad_unit = grad_rows * gain_row
    return inverse * (
        grad_unit
        - jnp.mean(grad_unit, axis=-1, keepdims=True)
        - unit_rows * jnp.mean(grad_unit * unit_rows, axis=-1, keepdims=True)
    )


def row_sum(value):
    return jnp.sum(value, axis=0, keepdims=True)


def aligned(index, size):
    return pl.ds(pl.multiple_of(index * size, size), size)


def kernel(
    x_ref, cot_ref, seg_ref, qkv_ref, wo_ref, fc1_ref, fc2_ref, gain_ref, offset_ref, qv_ref, proj_ref, fc_ref,
    out_ref, grad_ref, wgrad_ref, late_ref, early_ref,
    w, gd, r0, r1, r2, rq, p1, pb,
    g1, g2, gm, ga, sbuf, rbuf,
    qkv_s, prob_s, mixed_s, active_s, slope_s, unit_s, inv_s, mid_s,
    gb_s, gp_s, gx_s, gt_s, mask_s, dy_s, xs, xr,
    late, early, late_c, late_x, late_y, late_z, early_c, early_x, early_y, early_z,
    z_send, z_recv, gy_send, gy_recv, gx_send, gx_recv, gc_send, gc_recv,
    rc_send, rc_recv, rx_send, rx_recv, ry_send, ry_recv, o_send, o_recv, a_send, a_recv,
):
    s = lax.axis_index("section")
    d = lax.axis_index("dp")
    t = lax.axis_index("tensor")
    x = d // 4
    yl = (d // 2) % 2
    c = d % 2
    y = 2 * s + yl
    mate = {"section": s, "dp": d + 1 - 2 * c, "tensor": t}
    zp = [{"section": s, "dp": d, "tensor": (t + k) % 4} for k in (1, 2, 3)]
    xp = [{"section": s, "dp": ((x + k) % 4) * 4 + yl * 2 + c, "tensor": t} for k in (1, 2, 3)]
    yp = []
    for k in (1, 2, 3):
        other = (y + k) % 4
        yp.append({"section": other // 2, "dp": x * 4 + (other % 2) * 2 + c, "tensor": t})
    pair = {"section": s, "dp": x * 4 + (1 - yl) * 2 + c, "tensor": t}
    beyond = {"section": 1 - s, "dp": x * 4 + (1 - yl) * 2 + c, "tensor": t}
    across = {"section": 1 - s, "dp": d, "tensor": t}

    def remote(src, dst, send, recv, peer):
        return pltpu.make_async_remote_copy(
            src_ref=src, dst_ref=dst, send_sem=send, recv_sem=recv, device_id=peer, device_id_type=MESH
        )

    pending = {}

    def begin(key, copy, cond=None):
        if cond is None:
            copy.start()
        else:
            pl.when(cond)(copy.start)
        pending.setdefault(key, []).append((copy, cond))

    def flush(key):
        for copy, cond in pending.pop(key, []):
            if cond is None:
                copy.wait_send()
            else:
                pl.when(cond)(copy.wait_send)

    barrier = pltpu.get_barrier_semaphore()
    for peer in zp + xp + yp + [mate]:
        pl.semaphore_signal(barrier, inc=1, device_id=peer, device_id_type=MESH)
    pl.semaphore_wait(barrier, 10)

    def cols(g):
        return pl.ds(*GATHER[g])

    def near(g):
        return pl.ds(REDUCE[g][0] - 2560, REDUCE[g][1])

    def wcols(g):
        return pl.ds(*REDUCE[g])

    def own(g):
        return w.at[s, x, yl, c, :, cols(g)]

    def rows(h):
        return slice(h * HALF, (h + 1) * HALF)

    def part(h):
        return pl.ds(h * HALF, HALF)

    def gather_y(g):
        for k in (1, 2, 3):
            begin("gy", remote(
                own(g), own(g),
                gy_send.at[g, k - 1], gy_recv.at[s, g, k - 1], yp[k - 1],
            ))

    @scoped("gather_x")
    def gather_x(l, g):
        for k in (1, 2, 3):
            src_y = (y - k + 4) % 4
            copy = remote(
                own(g), w.at[l, x, src_y % 2, c, :, cols(g)],
                gy_send.at[g, k - 1], gy_recv.at[l, g, k - 1], yp[k - 1],
            )
            pl.when(src_y // 2 == l)(copy.wait_recv)
        mine = w.at[l, x, :, c, :, cols(g)]
        for k in (1, 2, 3):
            begin("gx", remote(mine, mine, gx_send.at[l, g, k - 1], gx_recv.at[l, g, k - 1], xp[k - 1]))

    @scoped("gather_c")
    def gather_c(l, g):
        for k in (1, 2, 3):
            theirs = w.at[l, (x - k + 4) % 4, :, c, :, cols(g)]
            remote(theirs, theirs, gx_send.at[l, g, k - 1], gx_recv.at[l, g, k - 1], xp[k - 1]).wait_recv()
        half = w.at[l, :, :, c, :, cols(g)]
        begin("gc", remote(half, half, gc_send.at[l, g], gc_recv.at[l, g], mate))

    def turn_x(g):
        for k in (1, 2, 3):
            begin("gx", remote(
                own(g), own(g),
                gx_send.at[0, g, k - 1], gx_recv.at[0, g, k - 1], xp[k - 1],
            ))

    @scoped("turn_y")
    def turn_y(g):
        for k in (1, 2, 3):
            remote(
                own(g), w.at[s, (x - k + 4) % 4, yl, c, :, cols(g)],
                gx_send.at[0, g, k - 1], gx_recv.at[0, g, k - 1], xp[k - 1],
            ).wait_recv()
        mine = w.at[s, :, yl, c, :, cols(g)]
        for k in (1, 2, 3):
            begin("gy", remote(mine, mine, gy_send.at[g, k - 1], gy_recv.at[s, g, k - 1], yp[k - 1]))

    @scoped("turn_c")
    def turn_c(l, g):
        for k in (1, 2, 3):
            src_y = (y - k + 4) % 4
            theirs = w.at[l, :, src_y % 2, c, :, cols(g)]
            copy = remote(theirs, theirs, gy_send.at[g, k - 1], gy_recv.at[l, g, k - 1], yp[k - 1])
            pl.when(src_y // 2 == l)(copy.wait_recv)
        half = w.at[l, :, :, c, :, cols(g)]
        begin("gc", remote(half, half, gc_send.at[l, g], gc_recv.at[l, g], mate))

    @scoped("gather_done")
    def gather_done(l, g):
        half = w.at[l, :, :, 1 - c, :, cols(g)]
        remote(half, half, gc_send.at[l, g], gc_recv.at[l, g], mate).wait_recv()

    def c_copy(l, g, step):
        at = (x + step) % 4
        return remote(
            gd.at[at, :, 1 - c, :, wcols(g)], r0.at[l, at, :, :, wcols(g)],
            rc_send.at[l, g, step], rc_recv.at[l, g, step], mate,
        )

    @scoped("reduce_c")
    def reduce_c(l, g, step):
        c_copy(l, g, step).wait_recv()
        at = (x + step) % 4
        for half in BOTH:
            gd[at, half, c, :, wcols(g)] = (
                gd[at, half, c, :, wcols(g)].astype(F32) + r0[l, at, half, :, wcols(g)].astype(F32)
            ).astype(BF16)
        if y_first(l, g):
            if step == 0:
                begin(("rx", l, g), wide_pair(l, g))
            return
        for i in {2: (0, 1), 1: (2,), 3: (3,), 0: ()}[step]:
            begin(("rx", l, g), x_copy(l, g, i))

    def x_copy(l, g, i):
        step, half = ((2, 0), (2, 1), (1, 1), (3, 0), (1, 0), (3, 1))[i]
        return remote(
            gd.at[(x + step) % 4, half, c, :, wcols(g)], r1.at[l, i, :, wcols(g)],
            rx_send.at[l, g, i], rx_recv.at[l, g, i], xp[2 * (i % 2)],
        )

    @scoped("reduce_f")
    def reduce_f(l, g):
        for i in BOTH:
            x_copy(l, g, i).wait_recv()
            at = (x + 1 + 2 * i) % 4
            gd[at, i, c, :, wcols(g)] = (
                gd[at, i, c, :, wcols(g)].astype(F32) + r1[l, i, :, wcols(g)].astype(F32)
            ).astype(BF16)
            begin(("rx", l, g), x_copy(l, g, 4 + i))

    @scoped("reduce_y")
    def reduce_y(l, g):
        for i in (2, 3, 4, 5):
            x_copy(l, g, i).wait_recv()
        for half in BOTH:
            total = gd[x, half, c, :, wcols(g)].astype(F32)
            for i in ((3, 4), (2, 5))[half]:
                total += r1[l, i, :, wcols(g)].astype(F32)
            p1[l, half, :, wcols(g)] = total.astype(BF16)
        if direct(l, g):
            for k in (1, 2, 3):
                target = (y + k) % 4
                begin("ry", remote(
                    p1.at[l, target % 2, :, wcols(g)], r2.at[l, k - 1, :, wcols(g)],
                    ry_send.at[l, g, k - 1], ry_recv.at[l, g, k - 1], yp[k - 1],
                ), target // 2 == l)
        else:
            begin("ry", pair_copy(l, g))

    def y_first(l, g):
        return l == 0 and g > 3

    def wide_pair(l, g):
        return remote(
            gd.at[:, (s + l + 1 + yl) % 2, c, :, wcols(g)], rq.at[0, :, :, near(g)],
            rx_send.at[l, g, 0], rx_recv.at[l, g, 0], pair,
        )

    def wide_cut(l, g):
        return remote(
            gd.at[:, 1 - yl, c, :, wcols(g)], rq.at[1, :, :, near(g)],
            rx_send.at[l, g, 1], rx_recv.at[l, g, 1], beyond,
        )

    def last_x(l, g, k):
        return remote(
            gd.at[(x + k) % 4, yl, c, :, wcols(g)], r1.at[l, k - 1, :, wcols(g)],
            rx_send.at[l, g, k + 1], rx_recv.at[l, g, k + 1], xp[k - 1],
        )

    @scoped("wide_y")
    def wide_y(l, g):
        @pl.when(s != l)
        def _():
            wide_pair(l, g).wait_recv()

            def add(i, _):
                gd[i, 1 - yl, c, :, wcols(g)] = (
                    gd[i, 1 - yl, c, :, wcols(g)].astype(F32) + rq[0, i, :, near(g)].astype(F32)
                ).astype(BF16)
                return 0

            lax.fori_loop(0, 4, add, 0)

        begin(("rx", l, g), wide_cut(l, g), s != l)

    @scoped("wide_x")
    def wide_x(l, g):
        @pl.when(s == l)
        def _():
            wide_pair(l, g).wait_recv()
            wide_cut(l, g).wait_recv()

            def add(i, _):
                gd[i, yl, c, :, wcols(g)] = (
                    gd[i, yl, c, :, wcols(g)].astype(F32)
                    + rq[0, i, :, near(g)].astype(F32)
                    + rq[1, i, :, near(g)].astype(F32)
                ).astype(BF16)
                return 0

            lax.fori_loop(0, 4, add, 0)

        for k in (1, 2, 3):
            begin(("rx", l, g), last_x(l, g, k), s == l)

    @scoped("wide_done")
    def wide_done(l, g):
        @pl.when(s == l)
        def _():
            for k in (1, 2, 3):
                last_x(l, g, k).wait_recv()
            total = gd[x, yl, c, :, wcols(g)].astype(F32)
            for k in (0, 1, 2):
                total += r1[l, k, :, wcols(g)].astype(F32)
            wgrad_ref[:, wcols(g)] = total

    def direct(l, g):
        return l == 0 and g < 2

    def pair_copy(l, g):
        return remote(
            p1.at[l, (s + l + 1 + yl) % 2, :, wcols(g)], r2.at[l, 0, :, wcols(g)],
            ry_send.at[l, g, 0], ry_recv.at[l, g, 0], pair,
        )

    def cut_copy(l, g):
        return remote(
            p1.at[l, 1 - yl, :, wcols(g)], r2.at[l, 1, :, wcols(g)],
            ry_send.at[l, g, 1], ry_recv.at[l, g, 1], beyond,
        )

    @scoped("reduce_g")
    def reduce_g(l, g):
        @pl.when(s != l)
        def _():
            pair_copy(l, g).wait_recv()
            p1[l, 1 - yl, :, wcols(g)] = (
                p1[l, 1 - yl, :, wcols(g)].astype(F32) + r2[l, 0, :, wcols(g)].astype(F32)
            ).astype(BF16)

        begin("ry", cut_copy(l, g), s != l)

    @scoped("reduce_done")
    def reduce_done(l, g):
        if direct(l, g):
            copies = [
                remote(
                    p1.at[l, 0, :, wcols(g)], r2.at[l, k, :, wcols(g)],
                    ry_send.at[l, g, k], ry_recv.at[l, g, k], yp[k],
                )
                for k in (0, 1, 2)
            ]
        else:
            copies = [pair_copy(l, g), cut_copy(l, g)]

        @pl.when(s == l)
        def _():
            for copy in copies:
                copy.wait_recv()
            total = p1[l, yl, :, wcols(g)].astype(F32)
            for k in range(len(copies)):
                total += r2[l, k, :, wcols(g)].astype(F32)
            wgrad_ref[:, wcols(g)] = total

    def spread_start(event, buf, h):
        mine = buf.at[t, part(h)]
        for k in (1, 2, 3):
            begin("z", remote(mine, mine, z_send.at[event, h, k - 1], z_recv.at[event, h, k - 1], zp[k - 1]))

    @scoped("spread_done")
    def spread_done(event, buf, h):
        for k in (1, 2, 3):
            theirs = buf.at[(t - k + 4) % 4, part(h)]
            remote(theirs, theirs, z_send.at[event, h, k - 1], z_recv.at[event, h, k - 1], zp[k - 1]).wait_recv()

    def sum_copy(event, h, k):
        return remote(
            sbuf.at[(event // 2) % 3, (t + k) % 4, part(h)], rbuf.at[event // 2, k - 1, part(h)],
            z_send.at[event, h, k - 1], z_recv.at[event, h, k - 1], zp[k - 1],
        )

    def sum_start(event, h):
        for k in (1, 2, 3):
            begin(("s", (event // 2) % 3, h), sum_copy(event, h, k))

    @scoped("sum_done")
    def sum_done(event, h):
        for k in (1, 2, 3):
            sum_copy(event, h, k).wait_recv()
        total = sbuf[(event // 2) % 3, t, rows(h)].astype(F32)
        for k in (0, 1, 2):
            total += rbuf[event // 2, k, rows(h)].astype(F32)
        return total

    @scoped("share")
    def share(event, h, lhs, l, c0, n):
        slot = (event // 2) % 3
        flush(("s", slot, h))

        def tile(j, _):
            right = w[l, j, :, :, :, pl.ds(c0, n)].reshape(256, n)
            value = dot_nt(lhs().reshape(4 * HALF, n), right).astype(BF16)
            sbuf[slot, :, rows(h), aligned(j, 256)] = value.reshape(4, HALF, 256)
            return 0

        lax.fori_loop(0, 4, tile, 0)
        sum_start(event, h)

    fills = []

    def fill(count):
        for _ in range(min(count, len(fills))):
            fills.pop(0)()

    def weight_grad(l, parts, lhs_ref, rhs_ref):
        c0, n = REDUCE[parts[0]][0], sum(REDUCE[g][1] for g in parts)

        @scoped("weight_grad")
        def one(step):
            at = (x + step) % 4
            gt_s[...] = lhs_ref[:, :, aligned(at, 256)].reshape(SEQ, 256).T

            def tile(j, _):
                value = dot_nn(gt_s[...], rhs_ref[:, :, aligned(j, 256)].reshape(SEQ, 256))
                gd[at, :, :, :, pl.ds(pl.multiple_of(c0 + j * 256, 256), 256)] = value.astype(
                    BF16
                ).reshape(2, 2, ROWS, 256)
                return 0

            lax.fori_loop(0, n // 256, tile, 0)
            for g in parts:
                begin(("rc", l, g), c_copy(l, g, step))

        for step in (2, 1, 3, 0):
            fills.append(functools.partial(one, step))

    def reduce_all(l, g):
        for step in (2, 1, 3, 0):
            reduce_c(l, g, step)

    def cross_send(index, value, l, local_ref, h):
        @pl.when(s == l)
        def _():
            local_ref[s, rows(h)] = value

        @pl.when(s != l)
        def _():
            xs[index, rows(h)] = value

        begin("o", remote(
            xs.at[index, part(h)], xr.at[index, part(h)], o_send.at[index, h], o_recv.at[index, h], across
        ), s != l)

    stages = {
        "c": ((late_c, early_c), c, [mate], 0), "x": ((late_x, early_x), x, xp, 1),
        "y": ((late_y, early_y), y, yp, 4), "z": ((late_z, early_z), t, zp, 7),
    }

    def all_sum(kind, l, stage):
        bufs, _, peers, _ = stages[stage]
        value = bufs[kind][l, 0]
        for k in range(1, len(peers) + 1):
            value = value + bufs[kind][l, k]
        return value

    def all_start(kind, l, stage, before=None):
        bufs, me, peers, at = stages[stage]
        buf = bufs[kind]
        buf[l, me] = (late, early)[kind][l] if before is None else all_sum(kind, l, before)
        for k, peer in enumerate(peers):
            begin("a", remote(
                buf.at[l, me], buf.at[l, me], a_send.at[kind, l, at + k], a_recv.at[kind, l, at + k], peer
            ))

    @scoped("all_wait")
    def all_wait(kind, l, stage):
        bufs, me, peers, at = stages[stage]
        n = len(peers) + 1
        for k, peer in enumerate(peers):
            theirs = bufs[kind].at[l, (me - k - 1 + n) % n]
            remote(theirs, theirs, a_send.at[kind, l, at + k], a_recv.at[kind, l, at + k], peer).wait_recv()

    def all_next(kind, l, stage, following):
        all_wait(kind, l, stage)
        all_start(kind, l, following, stage)

    def small(l, row):
        return pb[l, row:row + 1]

    def norm_one(l, h, hidden):
        normed, unit, inverse = norm_rows(hidden, small(l, GAIN), small(l, OFFSET))
        unit_s[l, 0, rows(h)] = unit
        inv_s[l, 0, rows(h)] = inverse
        g1[l, t, rows(h)] = normed.astype(BF16)
        spread_start(4 * l, g1.at[l], h)
        mid_s[rows(h)] = hidden

    def project(l, h):
        left = g1[l, :, rows(h)].reshape(4 * HALF, D)
        for j in range(3):
            value = dot_nn(left, w[l, :, :, :, :, j * 256:(j + 1) * 256].reshape(D, 256))
            if j != 1:
                value = value + pb[l, QV + j // 2:QV + j // 2 + 1, aligned(t, 256)]
            qkv_s[l, :, rows(h), j * 256:(j + 1) * 256] = value.astype(BF16).reshape(4, HALF, 256)

    def head(l, j, n):
        return qkv_s[l, :, :, j * 256 + n * HD:j * 256 + (n + 1) * HD].reshape(SEQ, HD)

    @scoped("attend")
    def attend(l):
        for pair in range(2):
            mixed = []
            for n in (2 * pair, 2 * pair + 1):
                scores = dot_nt(head(l, 0, n), head(l, 1, n)) * 0.125
                scores = jnp.where(mask_s[...] > 0.5, scores, NEGATIVE)
                shifted = jnp.exp(scores - jnp.max(scores, axis=-1, keepdims=True))
                probs = shifted / jnp.sum(shifted, axis=-1, keepdims=True)
                prob_s[l, n] = probs
                mixed.append(dot_nn(probs.astype(BF16), head(l, 2, n)))
            both = jnp.concatenate(mixed, axis=1).astype(BF16)
            mixed_s[l, :, :, pair * 128:(pair + 1) * 128] = both.reshape(4, ROWS, 128)

    def norm_two(l, h):
        middle = mid_s[rows(h)] + (sum_done(4 * l + 1, h) + small(l, PROJ))
        normed, unit, inverse = norm_rows(middle, small(l, GAIN + 1), small(l, OFFSET + 1))
        unit_s[l, 1, rows(h)] = unit
        inv_s[l, 1, rows(h)] = inverse
        g2[l, t, rows(h)] = normed.astype(BF16)
        spread_start(4 * l + 2, g2.at[l], h)
        mid_s[rows(h)] = middle

    @scoped("up")
    def up(l, h):
        def tile(j, _):
            at = aligned(j, 256)
            before = dot_nn(
                g2[l, :, rows(h)].reshape(4 * HALF, D),
                w[l, :, :, :, :, pl.ds(pl.multiple_of(1024 + j * 256, 256), 256)].reshape(D, 256),
            ) + pb[l, pl.ds(FC + t, 1), at]
            tanh_part = jnp.tanh(GELU_COEF * (before + 0.044715 * before * before * before))
            active = (0.5 * before * (1.0 + tanh_part)).astype(BF16)
            slope = 0.5 * (1.0 + tanh_part) + 0.5 * before * (
                1.0 - tanh_part * tanh_part
            ) * GELU_COEF * (1.0 + 3.0 * 0.044715 * before * before)
            active_s[l, :, rows(h), at] = active.reshape(4, HALF, 256)
            if l == 0:
                slope_s[l, :, rows(h), at] = slope.reshape(4, HALF, 256)
            else:
                grad_before = slope_s[l, :, rows(h), at].reshape(4 * HALF, 256) * slope
                early[l, pl.ds(4 + t, 1), at] += row_sum(grad_before)
                gb_s[:, rows(h), at] = grad_before.astype(BF16).reshape(4, HALF, 256)
            return 0

        lax.fori_loop(0, 4, tile, 0)

    def layer_out(l, h):
        return mid_s[rows(h)] + (sum_done(4 * l + 3, h) + small(l, PROJ + 1))

    def attention_part(l):
        for h in BOTH:
            spread_done(4 * l, g1.at[l], h)
            if h == 0:
                gather_done(l, 0)
            project(l, h)
        gather_c(l, 1)
        attend(l)
        gather_done(l, 1)
        for h in BOTH:
            share(4 * l + 1, h, lambda h=h: mixed_s[l, :, rows(h)], l, 768, 256)

    @scoped("before_up")
    def before_up(l):
        def tile(j, _):
            value = dot_nn(
                gm[l].reshape(SEQ, D),
                w[l, :, :, :, :, pl.ds(pl.multiple_of(2048 + j * 256, 256), 256)].reshape(D, 256),
            )
            slope_s[l, :, :, aligned(j, 256)] = value.reshape(4, ROWS, 256)
            return 0

        lax.fori_loop(0, 4, tile, 0)

    @scoped("down")
    def down(l, h):
        def tile(j, _):
            at = aligned(j, 256)
            grad_before = dot_nn(
                gm[l, :, rows(h)].reshape(4 * HALF, D),
                w[l, :, :, :, :, pl.ds(pl.multiple_of(2048 + j * 256, 256), 256)].reshape(D, 256),
            ) * slope_s[l, :, rows(h), at].reshape(4 * HALF, 256)
            early[l, pl.ds(4 + t, 1), at] += row_sum(grad_before)
            gb_s[:, rows(h), at] = grad_before.astype(BF16).reshape(4, HALF, 256)
            return 0

        lax.fori_loop(0, 4, tile, 0)

    def norm_two_back(l, h):
        grad = sum_done(13 - 4 * l, h)
        unit = unit_s[l, 1, rows(h)]
        early[l, 0:1] += row_sum(grad * unit)
        early[l, 1:2] += row_sum(grad)
        grad_middle = dy_s[rows(h)] + norm_back(grad, unit, inv_s[l, 1, rows(h)], small(l, GAIN + 1))
        dy_s[rows(h)] = grad_middle
        ga[l, t, rows(h)] = grad_middle.astype(BF16)
        spread_start(14 - 4 * l, ga.at[l], h)
        early[l, 2:3] += row_sum(grad_middle)

    def mixed_back(l, h):
        value = dot_nn(
            ga[l, :, rows(h)].reshape(4 * HALF, D), w[l, :, :, :, :, 768:1024].reshape(D, 256)
        )
        gx_s[:, rows(h)] = value.astype(BF16).reshape(4, HALF, 256)

    @scoped("attend_back")
    def attend_back(l):
        for pair in range(2):
            grads = [[], [], []]
            for n in (2 * pair, 2 * pair + 1):
                q, key, value = head(l, 0, n), head(l, 1, n), head(l, 2, n)
                grad_head = gx_s[:, :, n * HD:(n + 1) * HD].reshape(SEQ, HD)
                probs = prob_s[l, n]
                grad_probs = dot_nt(grad_head, value)
                row_dot = jnp.sum(probs * grad_probs, axis=-1, keepdims=True)
                grad_scores = (probs * (grad_probs - row_dot)).astype(BF16)
                grads[0].append(dot_nn(grad_scores, key) * 0.125)
                grads[1].append(dot_tn(grad_scores, q) * 0.125)
                grads[2].append(dot_tn(probs.astype(BF16), grad_head))
            for j in range(3):
                both = jnp.concatenate(grads[j], axis=1)
                gp_s[:, :, j * 256 + pair * 128:j * 256 + (pair + 1) * 128] = both.astype(BF16).reshape(
                    4, ROWS, 128
                )
                if j != 1:
                    total = row_sum(both)
                    for k in BOTH:
                        late[l, 4 + j + k:5 + j + k, aligned((t % 2) * 2 + pair, 128)] = jnp.where(
                            t // 2 == k, total, 0.0
                        )

    def norm_one_back(l, h):
        grad = sum_done(15 - 4 * l, h)
        unit = unit_s[l, 0, rows(h)]
        for row, value in ((0, row_sum(grad * unit)), (2, row_sum(grad))):
            late[l, row:row + 1] += value[:, :512]
            late[l, row + 1:row + 2] += value[:, 512:]
        return dy_s[rows(h)] + norm_back(grad, unit, inv_s[l, 0, rows(h)], small(l, GAIN))

    pb[s, GAIN:GAIN + 2] = gain_ref[...]
    pb[s, OFFSET:OFFSET + 2] = offset_ref[...]
    pb[s, PROJ:PROJ + 2] = proj_ref[...]
    pb[s, QV:QV + 2] = qv_ref[...]
    for k in range(4):
        pb[s, FC + k:FC + k + 1] = fc_ref[:, k * 1024:(k + 1) * 1024]
    pb[s, FC + 4:] = jnp.zeros((SMALL - FC - 4, D), F32)
    for j in range(3):
        w[s, x, yl, c, :, j * 256:(j + 1) * 256] = qkv_ref[j]
    gather_y(0)
    w[s, x, yl, c, :, 768:1024] = wo_ref[...]
    gather_y(1)
    w[s, x, yl, c, :, 2048:] = fc2_ref[...]
    turn_x(5)
    begin("pb", remote(pb.at[s], pb.at[s], o_send.at[4, 0], o_recv.at[4, 0], across))
    w[s, x, yl, c, :, 1024:2048] = fc1_ref[...]
    late[...] = jnp.zeros_like(late)
    early[...] = jnp.zeros_like(early)
    seg_rows = jnp.broadcast_to(seg_ref[s].astype(F32), (SEQ, SEQ))
    seg_cols = seg_rows.T
    places_i = lax.broadcasted_iota(jnp.int32, (SEQ, SEQ), 0)
    places_j = lax.broadcasted_iota(jnp.int32, (SEQ, SEQ), 1)
    mask_s[...] = jnp.where((seg_rows == seg_cols) & (places_i >= places_j), 1.0, 0.0)
    gather_x(0, 0)
    gather_y(2)
    gather_x(0, 1)
    gather_y(3)
    gather_y(4)
    turn_y(5)
    with jax.named_scope("wait_pb"):
        remote(pb.at[1 - s], pb.at[1 - s], o_send.at[4, 0], o_recv.at[4, 0], across).wait_recv()
    for h in BOTH:
        norm_one(0, h, x_ref[s, rows(h)].astype(F32))
    gm[1, t] = cot_ref[s]
    for h in BOTH:
        spread_start(8, gm.at[1], h)
    dy_s[...] = cot_ref[s].astype(F32)
    early[1, 3:4] = row_sum(dy_s[...])
    gather_c(0, 0)
    for g in (2, 3, 4):
        gather_x(0, g)

    attention_part(0)
    gather_c(0, 2)
    gather_x(1, 0)
    gather_x(1, 1)
    for h in BOTH:
        norm_two(0, h)
    gather_c(0, 3)
    gather_c(0, 4)
    turn_c(0, 5)
    for h in BOTH:
        spread_done(2, g2.at[0], h)
        if h == 0:
            gather_done(0, 2)
            gather_done(0, 3)
        up(0, h)
        if h == 0:
            gather_done(0, 4)
            gather_done(0, 5)
        share(3, h, lambda h=h: active_s[0, :, rows(h)], 0, 2048, 1024)
    gather_x(1, 4)
    gather_x(1, 2)
    for h in BOTH:
        hidden = layer_out(0, h)
        norm_one(1, h, hidden.astype(BF16).astype(F32))
        cross_send(0, hidden, 0, out_ref, h)
        if h == 0:
            gather_c(1, 0)
    gather_x(1, 3)
    turn_c(1, 5)

    attention_part(1)
    for h in BOTH:
        spread_done(8, gm.at[1], h)
    gather_c(1, 4)
    gather_done(1, 5)
    gather_c(1, 2)
    gather_done(1, 4)
    before_up(1)
    for h in BOTH:
        norm_two(1, h)
    gather_c(1, 3)
    weight_grad(1, (3, 4), gm.at[1], active_s.at[1])
    weight_grad(1, (2,), g2.at[1], gb_s)
    for h in BOTH:
        spread_done(6, g2.at[1], h)
        if h == 0:
            gather_done(1, 2)
            gather_done(1, 3)
        up(1, h)
        share(9, h, lambda h=h: gb_s[:, rows(h)], 1, 1024, 1024)
    fill(4)
    norm_two_back(1, 0)
    fill(2)
    norm_two_back(1, 1)
    fill(1)
    reduce_all(1, 3)
    reduce_all(1, 4)
    fill(1)
    share(7, 0, lambda: active_s[1, :, rows(0)], 1, 2048, 1024)
    spread_done(10, ga.at[1], 0)
    mixed_back(1, 0)
    share(7, 1, lambda: active_s[1, :, rows(1)], 1, 2048, 1024)
    spread_done(10, ga.at[1], 1)
    mixed_back(1, 1)
    attend_back(1)
    for h in BOTH:
        share(11, h, lambda h=h: gp_s[:, rows(h)], 1, 0, 768)
    reduce_all(1, 2)
    reduce_f(1, 3)
    reduce_f(1, 4)
    weight_grad(1, (0,), g1.at[1], gp_s)
    weight_grad(1, (1,), ga.at[1], mixed_s.at[1])
    fill(8)

    def pass_grad(h):
        grad = norm_one_back(1, h).astype(BF16)
        gm[0, t, rows(h)] = grad
        spread_start(12, gm.at[0], h)
        dy_s[rows(h)] = grad.astype(F32)
        cross_send(3, grad.astype(F32), 1, grad_ref, h)

    pass_grad(0)
    for h in BOTH:
        hidden = layer_out(1, h)
        cross_send(2, hidden, 1, out_ref, h)
    pass_grad(1)
    reduce_f(1, 2)
    reduce_all(1, 0)
    early[0, 3:4] = row_sum(dy_s[...])
    for kind in BOTH:
        all_start(kind, 1, "c")

    for h in BOTH:
        spread_done(12, gm.at[0], h)
        down(0, h)
        share(13, h, lambda h=h: gb_s[:, rows(h)], 0, 1024, 1024)
    for kind in BOTH:
        all_next(kind, 1, "c", "y")
    reduce_all(1, 1)
    reduce_y(1, 3)
    reduce_y(1, 4)
    for g in (4, 3, 2):
        flush(("rc", 1, g))
        flush(("rx", 1, g))
    weight_grad(0, (3, 4), gm.at[0], active_s.at[0])
    weight_grad(0, (2,), g2.at[0], gb_s)
    fill(4)
    reduce_f(1, 0)
    norm_two_back(0, 0)
    reduce_y(1, 2)
    fill(2)
    norm_two_back(0, 1)
    reduce_f(1, 1)
    reduce_all(0, 4)
    reduce_all(0, 3)
    fill(2)
    reduce_g(1, 3)
    reduce_g(1, 4)
    spread_done(14, ga.at[0], 0)
    mixed_back(0, 0)
    reduce_g(1, 2)
    reduce_y(1, 0)
    for kind in BOTH:
        all_next(kind, 1, "y", "x")
    spread_done(14, ga.at[0], 1)
    mixed_back(0, 1)
    reduce_all(0, 2)
    attend_back(0)
    for h in BOTH:
        share(15, h, lambda h=h: gp_s[:, rows(h)], 0, 0, 768)
    all_start(1, 0, "c")
    reduce_y(1, 1)
    for g in (1, 0):
        flush(("rc", 1, g))
        flush(("rx", 1, g))
    weight_grad(0, (1,), ga.at[0], mixed_s.at[0])
    fill(4)
    wide_y(0, 4)
    reduce_f(0, 3)
    reduce_g(1, 0)
    weight_grad(0, (0,), g1.at[0], gp_s)
    fill(3)
    reduce_all(0, 1)
    fill(1)
    all_next(1, 0, "c", "y")
    reduce_c(0, 0, 2)
    reduce_f(0, 2)
    for step in (1, 3, 0):
        reduce_c(0, 0, step)
    reduce_g(1, 1)
    cross_send(1, norm_one_back(0, 0), 0, grad_ref, 0)
    for kind in BOTH:
        all_next(kind, 1, "x", "z")
    cross_send(1, norm_one_back(0, 1), 0, grad_ref, 1)
    all_start(0, 0, "c")
    all_next(0, 0, "c", "z")
    reduce_y(0, 3)
    all_next(0, 0, "z", "y")
    reduce_f(0, 1)
    reduce_f(0, 0)
    reduce_y(0, 2)
    all_next(1, 0, "y", "x")
    wide_x(0, 4)
    reduce_g(0, 3)
    all_next(0, 0, "y", "x")
    reduce_y(0, 1)
    reduce_y(0, 0)
    all_next(1, 0, "x", "z")
    reduce_g(0, 2)
    for g in (4, 3, 2, 1, 0):
        reduce_done(1, g)
    for kind in BOTH:
        all_wait(kind, 1, "z")
    all_wait(0, 0, "x")
    all_wait(1, 0, "z")
    for kind, ref in ((0, late_ref), (1, early_ref)):
        ref[...] = jnp.where(s == 0, all_sum(kind, 0, "zx"[1 - kind]), all_sum(kind, 1, "z"))
    for ref, pairs in ((out_ref, (0, 2)), (grad_ref, (1, 3))):
        for h in BOTH:
            first, second = [
                remote(
                    xs.at[index, part(h)], xr.at[index, part(h)], o_send.at[index, h], o_recv.at[index, h], across
                )
                for index in pairs
            ]
            pl.when(s == 0)(first.wait_recv)
            pl.when(s == 1)(second.wait_recv)

        @pl.when(s == 0)
        def _():
            ref[1 - s] = xr[pairs[0]]

        @pl.when(s == 1)
        def _():
            ref[1 - s] = xr[pairs[1]]

    wide_done(0, 4)
    for g in (3, 2, 1, 0):
        reduce_done(0, g)
    for key in list(pending):
        flush(key)


def finish(
    out_ref, grad_ref, wgrad_ref, late_ref, early_ref,
    outs, grads, qkv, out, fc1, fc2, gain, offset, qv, proj, fc,
):
    outs[0] = out_ref[...]
    grads[0] = grad_ref[...]
    for j in range(3):
        qkv[0, j] = wgrad_ref[:, j * 256:(j + 1) * 256]
    out[0] = wgrad_ref[:, 768:1024]
    fc1[0] = wgrad_ref[:, 1024:2048]
    fc2[0] = wgrad_ref[:, 2048:]
    for ref, row, other in ((gain, 0, 0), (offset, 2, 1)):
        for k in BOTH:
            ref[0, 0:1, k * 512:(k + 1) * 512] = late_ref[row + k:row + k + 1]
        ref[0, 1:2] = early_ref[other:other + 1]
    for row in BOTH:
        for k in BOTH:
            at = 4 + 2 * row + k
            qv[0, row:row + 1, k * 512:(k + 1) * 512] = late_ref[at:at + 1]
    proj[0] = early_ref[2:4]
    for k in range(4):
        fc[:, k * 1024:(k + 1) * 1024] = early_ref[4 + k:5 + k]


def fused(*args):
    vmem = pl.BlockSpec(memory_space=pltpu.VMEM)
    dma = pltpu.SemaphoreType.DMA
    scratch = [
        pltpu.VMEM((2, 4, 2, 2, ROWS, WIDE), BF16),
        pltpu.VMEM((4, 2, 2, ROWS, WIDE), BF16),
        pltpu.VMEM((2, 4, 2, ROWS, WIDE), BF16),
        pltpu.VMEM((2, 6, ROWS, WIDE), BF16),
        pltpu.VMEM((2, 3, ROWS, WIDE), BF16),
        pltpu.VMEM((2, 4, ROWS, 512), BF16),
        pltpu.VMEM((2, 2, ROWS, WIDE), BF16),
        pltpu.VMEM((2, SMALL, D), F32),
        pltpu.VMEM((2, 4, ROWS, D), BF16),
        pltpu.VMEM((2, 4, ROWS, D), BF16),
        pltpu.VMEM((2, 4, ROWS, D), BF16),
        pltpu.VMEM((2, 4, ROWS, D), BF16),
        pltpu.VMEM((3, 4, ROWS, D), BF16),
        pltpu.VMEM((8, 3, ROWS, D), BF16),
        pltpu.VMEM((2, 4, ROWS, 768), BF16),
        pltpu.VMEM((2, 4, SEQ, SEQ), F32),
        pltpu.VMEM((2, 4, ROWS, 256), BF16),
        pltpu.VMEM((2, 4, ROWS, D), BF16),
        pltpu.VMEM((2, 4, ROWS, D), F32),
        pltpu.VMEM((2, 2, ROWS, D), F32),
        pltpu.VMEM((2, 2, ROWS, 1), F32),
        pltpu.VMEM((ROWS, D), F32),
        pltpu.VMEM((4, ROWS, D), BF16),
        pltpu.VMEM((4, ROWS, 768), BF16),
        pltpu.VMEM((4, ROWS, 256), BF16),
        pltpu.VMEM((256, SEQ), BF16),
        pltpu.VMEM((SEQ, SEQ), F32),
        pltpu.VMEM((ROWS, D), F32),
        pltpu.VMEM((4, ROWS, D), F32),
        pltpu.VMEM((4, ROWS, D), F32),
        pltpu.VMEM((2, 8, 512), F32),
        pltpu.VMEM((2, 8, D), F32),
    ]
    for width in (512, D):
        scratch += [pltpu.VMEM((2, n, 8, width), F32) for n in (2, 4, 4, 4)]
    scratch += [
        dma((16, 2, 3)), dma((16, 2, 3)),
        dma((6, 3)), dma((2, 6, 3)),
        dma((2, 6, 3)), dma((2, 6, 3)),
        dma((2, 6)), dma((2, 6)),
        dma((2, 5, 4)), dma((2, 5, 4)),
        dma((2, 5, 6)), dma((2, 5, 6)),
        dma((2, 5, 3)), dma((2, 5, 3)),
        dma((5, 2)), dma((5, 2)),
        dma((2, 2, 10)), dma((2, 2, 10)),
    ]
    sums = pl.pallas_call(
        kernel,
        out_shape=(
            jax.ShapeDtypeStruct((2, ROWS, D), F32),
            jax.ShapeDtypeStruct((2, ROWS, D), F32),
            jax.ShapeDtypeStruct((ROWS, WIDE), F32),
            jax.ShapeDtypeStruct((8, 512), F32),
            jax.ShapeDtypeStruct((8, D), F32),
        ),
        in_specs=[vmem] * 12,
        out_specs=(vmem,) * 5,
        scratch_shapes=scratch,
        compiler_params=pltpu.CompilerParams(
            collective_id=0, has_side_effects=True, vmem_limit_bytes=62 * 2**20
        ),
    )(*args)
    return pl.pallas_call(
        finish,
        out_shape=(
            jax.ShapeDtypeStruct((1, 2, ROWS, D), F32),
            jax.ShapeDtypeStruct((1, 2, ROWS, D), F32),
            jax.ShapeDtypeStruct((1, 3, ROWS, 256), F32),
            jax.ShapeDtypeStruct((1, ROWS, 256), F32),
            jax.ShapeDtypeStruct((1, ROWS, 1024), F32),
            jax.ShapeDtypeStruct((1, ROWS, 1024), F32),
            jax.ShapeDtypeStruct((1, 2, D), F32),
            jax.ShapeDtypeStruct((1, 2, D), F32),
            jax.ShapeDtypeStruct((1, 2, D), F32),
            jax.ShapeDtypeStruct((1, 2, D), F32),
            jax.ShapeDtypeStruct((1, FF), F32),
        ),
        in_specs=[vmem] * 5,
        out_specs=(vmem,) * 11,
    )(*sums)


def local(
    inputs, cotangent, segments, qkv_weight, out_weight, fc1_weight, fc2_weight,
    ln_gains, ln_biases, qv_bias, proj_biases, fc_bias,
):
    outs, grads, qkv, out, fc1, fc2, gain, offset, qv, proj, fc = fused(
        inputs, cotangent, segments,
        jnp.transpose(qkv_weight[0], (1, 0, 2)), out_weight[0].T, fc1_weight[0], fc2_weight[0].T,
        ln_gains[0], ln_biases[0], qv_bias[0], proj_biases[0], fc_bias,
    )
    return (
        outs, grads, jnp.transpose(qkv, (0, 2, 1, 3)), jnp.transpose(out, (0, 2, 1)), fc1,
        jnp.transpose(fc2, (0, 2, 1)), gain, offset, qv, proj, fc,
    )


def solution(mesh):
    in_specs = (
        P(None, ("dp", "tensor"), None),
        P(None, ("dp", "tensor"), None),
        P(None, "dp", None),
        P("section", "dp", None, "tensor"),
        P("section", "tensor", "dp"),
        P("section", "dp", "tensor"),
        P("section", "tensor", "dp"),
        P("section", None, None),
        P("section", None, None),
        P("section", None, None),
        P("section", None, None),
        P("section", None),
    )
    out_specs = (
        P("section", None, ("dp", "tensor"), None),
        P("section", None, ("dp", "tensor"), None),
        P("section", "dp", None, "tensor"),
        P("section", "tensor", "dp"),
        P("section", "dp", "tensor"),
        P("section", "tensor", "dp"),
        P("section", None, None),
        P("section", None, None),
        P("section", None, None),
        P("section", None, None),
        P("section", None),
    )
    return jax.shard_map(local, mesh=mesh, in_specs=in_specs, out_specs=out_specs, check_vma=False)
```

```python
import functools
import math

import jax
import jax.numpy as jnp
from jax import lax
from jax.experimental import pallas as pl
from jax.experimental.pallas import tpu as pltpu
from jax.sharding import PartitionSpec as P

D = 1024
HD = 64
FF = 4096
SEQ = 256
ROWS = 64
WIDE = 3072
NEGATIVE = -1000000000.0
GELU_COEF = 0.7978845608028654
EPSILON = 1e-05
MESH = pl.DeviceIdType.MESH
BF16 = jnp.bfloat16
F32 = jnp.float32

GAIN, OFFSET, PROJ, QV, FC = 0, 2, 4, 6, 8
SMALL = 16
HALF = ROWS // 2
BOTH = (0, 1)
GATHER = ((0, 768), (768, 256), (1024, 512), (1536, 512), (2048, 256), (2304, 768))
REDUCE = ((0, 768), (768, 256), (1024, 1024), (2048, 512), (2560, 512))


def scoped(name):
    def deco(func):
        def run(*args, **named):
            with jax.named_scope(name):
                return func(*args, **named)

        return run

    return deco


def dot_nn(a, b):
    return lax.dot_general(a, b, (((1,), (0,)), ((), ())), preferred_element_type=F32)


def dot_nt(a, b):
    return lax.dot_general(a, b, (((1,), (1,)), ((), ())), preferred_element_type=F32)


def dot_tn(a, b):
    return lax.dot_general(a, b, (((0,), (0,)), ((), ())), preferred_element_type=F32)


def norm_rows(hidden, gain_row, offset_row):
    centre = hidden - jnp.mean(hidden, axis=-1, keepdims=True)
    spread = jnp.mean(centre * centre, axis=-1, keepdims=True)
    inverse = lax.rsqrt(spread + EPSILON)
    unit_rows = centre * inverse
    return unit_rows * gain_row + offset_row, unit_rows, inverse


def norm_back(grad_rows, unit_rows, inverse, gain_row):
    grad_unit = grad_rows * gain_row
    return inverse * (
        grad_unit
        - jnp.mean(grad_unit, axis=-1, keepdims=True)
        - unit_rows * jnp.mean(grad_unit * unit_rows, axis=-1, keepdims=True)
    )


def row_sum(value):
    return jnp.sum(value, axis=0, keepdims=True)


def aligned(index, size):
    return pl.ds(pl.multiple_of(index * size, size), size)


def kernel(
    x_ref, cot_ref, seg_ref, qkv_ref, wo_ref, fc1_ref, fc2_ref, gain_ref, offset_ref, qv_ref, proj_ref, fc_ref,
    out_ref, grad_ref, wgrad_ref, late_ref, early_ref,
    w, gd, r0, r1, r2, rq, p1, pb,
    g1, g2, gm, ga, sbuf, rbuf,
    qkv_s, prob_s, mixed_s, active_s, slope_s, unit_s, inv_s, mid_s,
    gb_s, gp_s, gx_s, gt_s, mask_s, dy_s, xs, xr,
    late, early, late_c, late_x, late_y, late_z, early_c, early_x, early_y, early_z,
    z_send, z_recv, gy_send, gy_recv, gx_send, gx_recv, gc_send, gc_recv,
    rc_send, rc_recv, rx_send, rx_recv, ry_send, ry_recv, o_send, o_recv, a_send, a_recv,
):
    s = lax.axis_index("section")
    d = lax.axis_index("dp")
    t = lax.axis_index("tensor")
    x = d // 4
    yl = (d // 2) % 2
    c = d % 2
    y = 2 * s + yl
    mate = {"section": s, "dp": d + 1 - 2 * c, "tensor": t}
    zp = [{"section": s, "dp": d, "tensor": (t + k) % 4} for k in (1, 2, 3)]
    xp = [{"section": s, "dp": ((x + k) % 4) * 4 + yl * 2 + c, "tensor": t} for k in (1, 2, 3)]
    yp = []
    for k in (1, 2, 3):
        other = (y + k) % 4
        yp.append({"section": other // 2, "dp": x * 4 + (other % 2) * 2 + c, "tensor": t})
    pair = {"section": s, "dp": x * 4 + (1 - yl) * 2 + c, "tensor": t}
    beyond = {"section": 1 - s, "dp": x * 4 + (1 - yl) * 2 + c, "tensor": t}
    across = {"section": 1 - s, "dp": d, "tensor": t}

    def remote(src, dst, send, recv, peer):
        return pltpu.make_async_remote_copy(
            src_ref=src, dst_ref=dst, send_sem=send, recv_sem=recv, device_id=peer, device_id_type=MESH
        )

    pending = {}

    def begin(key, copy, cond=None):
        if cond is None:
            copy.start()
        else:
            pl.when(cond)(copy.start)
        pending.setdefault(key, []).append((copy, cond))

    def flush(key):
        for copy, cond in pending.pop(key, []):
            if cond is None:
                copy.wait_send()
            else:
                pl.when(cond)(copy.wait_send)

    barrier = pltpu.get_barrier_semaphore()
    for peer in zp + xp + yp + [mate]:
        pl.semaphore_signal(barrier, inc=1, device_id=peer, device_id_type=MESH)
    pl.semaphore_wait(barrier, 10)

    def cols(g):
        return pl.ds(*GATHER[g])

    def near(g):
        return pl.ds(REDUCE[g][0] - 2560, REDUCE[g][1])

    def wcols(g):
        return pl.ds(*REDUCE[g])

    def own(g):
        return w.at[s, x, yl, c, :, cols(g)]

    def rows(h):
        return slice(h * HALF, (h + 1) * HALF)

    def part(h):
        return pl.ds(h * HALF, HALF)

    def gather_y(g):
        for k in (1, 2, 3):
            begin("gy", remote(
                own(g), own(g),
                gy_send.at[g, k - 1], gy_recv.at[s, g, k - 1], yp[k - 1],
            ))

    @scoped("gather_x")
    def gather_x(l, g):
        for k in (1, 2, 3):
            src_y = (y - k + 4) % 4
            copy = remote(
                own(g), w.at[l, x, src_y % 2, c, :, cols(g)],
                gy_send.at[g, k - 1], gy_recv.at[l, g, k - 1], yp[k - 1],
            )
            pl.when(src_y // 2 == l)(copy.wait_recv)
        mine = w.at[l, x, :, c, :, cols(g)]
        for k in (1, 2, 3):
            begin("gx", remote(mine, mine, gx_send.at[l, g, k - 1], gx_recv.at[l, g, k - 1], xp[k - 1]))

    @scoped("gather_c")
    def gather_c(l, g):
        for k in (1, 2, 3):
            theirs = w.at[l, (x - k + 4) % 4, :, c, :, cols(g)]
            remote(theirs, theirs, gx_send.at[l, g, k - 1], gx_recv.at[l, g, k - 1], xp[k - 1]).wait_recv()
        half = w.at[l, :, :, c, :, cols(g)]
        begin("gc", remote(half, half, gc_send.at[l, g], gc_recv.at[l, g], mate))

    def turn_x(g):
        for k in (1, 2, 3):
            begin("gx", remote(
                own(g), own(g),
                gx_send.at[0, g, k - 1], gx_recv.at[0, g, k - 1], xp[k - 1],
            ))

    @scoped("turn_y")
    def turn_y(g):
        for k in (1, 2, 3):
            remote(
                own(g), w.at[s, (x - k + 4) % 4, yl, c, :, cols(g)],
                gx_send.at[0, g, k - 1], gx_recv.at[0, g, k - 1], xp[k - 1],
            ).wait_recv()
        mine = w.at[s, :, yl, c, :, cols(g)]
        for k in (1, 2, 3):
            begin("gy", remote(mine, mine, gy_send.at[g, k - 1], gy_recv.at[s, g, k - 1], yp[k - 1]))

    @scoped("turn_c")
    def turn_c(l, g):
        for k in (1, 2, 3):
            src_y = (y - k + 4) % 4
            theirs = w.at[l, :, src_y % 2, c, :, cols(g)]
            copy = remote(theirs, theirs, gy_send.at[g, k - 1], gy_recv.at[l, g, k - 1], yp[k - 1])
            pl.when(src_y // 2 == l)(copy.wait_recv)
        half = w.at[l, :, :, c, :, cols(g)]
        begin("gc", remote(half, half, gc_send.at[l, g], gc_recv.at[l, g], mate))

    @scoped("gather_done")
    def gather_done(l, g):
        half = w.at[l, :, :, 1 - c, :, cols(g)]
        remote(half, half, gc_send.at[l, g], gc_recv.at[l, g], mate).wait_recv()

    def c_copy(l, g, step):
        at = (x + step) % 4
        return remote(
            gd.at[at, :, 1 - c, :, wcols(g)], r0.at[l, at, :, :, wcols(g)],
            rc_send.at[l, g, step], rc_recv.at[l, g, step], mate,
        )

    @scoped("reduce_c")
    def reduce_c(l, g, step):
        c_copy(l, g, step).wait_recv()
        at = (x + step) % 4
        for half in BOTH:
            gd[at, half, c, :, wcols(g)] = (
                gd[at, half, c, :, wcols(g)].astype(F32) + r0[l, at, half, :, wcols(g)].astype(F32)
            ).astype(BF16)
        if y_first(l, g):
            if step == 0:
                begin(("rx", l, g), wide_pair(l, g))
            return
        for i in {2: (0, 1), 1: (2,), 3: (3,), 0: ()}[step]:
            begin(("rx", l, g), x_copy(l, g, i))

    def x_copy(l, g, i):
        step, half = ((2, 0), (2, 1), (1, 1), (3, 0), (1, 0), (3, 1))[i]
        return remote(
            gd.at[(x + step) % 4, half, c, :, wcols(g)], r1.at[l, i, :, wcols(g)],
            rx_send.at[l, g, i], rx_recv.at[l, g, i], xp[2 * (i % 2)],
        )

    @scoped("reduce_f")
    def reduce_f(l, g):
        for i in BOTH:
            x_copy(l, g, i).wait_recv()
            at = (x + 1 + 2 * i) % 4
            gd[at, i, c, :, wcols(g)] = (
                gd[at, i, c, :, wcols(g)].astype(F32) + r1[l, i, :, wcols(g)].astype(F32)
            ).astype(BF16)
            begin(("rx", l, g), x_copy(l, g, 4 + i))

    @scoped("reduce_y")
    def reduce_y(l, g):
        for i in (2, 3, 4, 5):
            x_copy(l, g, i).wait_recv()
        for half in BOTH:
            total = gd[x, half, c, :, wcols(g)].astype(F32)
            for i in ((3, 4), (2, 5))[half]:
                total += r1[l, i, :, wcols(g)].astype(F32)
            p1[l, half, :, wcols(g)] = total.astype(BF16)
        if direct(l, g):
            for k in (1, 2, 3):
                target = (y + k) % 4
                begin("ry", remote(
                    p1.at[l, target % 2, :, wcols(g)], r2.at[l, k - 1, :, wcols(g)],
                    ry_send.at[l, g, k - 1], ry_recv.at[l, g, k - 1], yp[k - 1],
                ), target // 2 == l)
        else:
            begin("ry", pair_copy(l, g))

    def y_first(l, g):
        return l == 0 and g > 3

    def wide_pair(l, g):
        return remote(
            gd.at[:, (s + l + 1 + yl) % 2, c, :, wcols(g)], rq.at[0, :, :, near(g)],
            rx_send.at[l, g, 0], rx_recv.at[l, g, 0], pair,
        )

    def wide_cut(l, g):
        return remote(
            gd.at[:, 1 - yl, c, :, wcols(g)], rq.at[1, :, :, near(g)],
            rx_send.at[l, g, 1], rx_recv.at[l, g, 1], beyond,
        )

    def last_x(l, g, k):
        return remote(
            gd.at[(x + k) % 4, yl, c, :, wcols(g)], r1.at[l, k - 1, :, wcols(g)],
            rx_send.at[l, g, k + 1], rx_recv.at[l, g, k + 1], xp[k - 1],
        )

    @scoped("wide_y")
    def wide_y(l, g):
        @pl.when(s != l)
        def _():
            wide_pair(l, g).wait_recv()

            def add(i, _):
                gd[i, 1 - yl, c, :, wcols(g)] = (
                    gd[i, 1 - yl, c, :, wcols(g)].astype(F32) + rq[0, i, :, near(g)].astype(F32)
                ).astype(BF16)
                return 0

            lax.fori_loop(0, 4, add, 0)

        begin(("rx", l, g), wide_cut(l, g), s != l)

    @scoped("wide_x")
    def wide_x(l, g):
        @pl.when(s == l)
        def _():
            wide_pair(l, g).wait_recv()
            wide_cut(l, g).wait_recv()

            def add(i, _):
                gd[i, yl, c, :, wcols(g)] = (
                    gd[i, yl, c, :, wcols(g)].astype(F32)
                    + rq[0, i, :, near(g)].astype(F32)
                    + rq[1, i, :, near(g)].astype(F32)
                ).astype(BF16)
                return 0

            lax.fori_loop(0, 4, add, 0)

        for k in (1, 2, 3):
            begin(("rx", l, g), last_x(l, g, k), s == l)

    @scoped("wide_done")
    def wide_done(l, g):
        @pl.when(s == l)
        def _():
            for k in (1, 2, 3):
                last_x(l, g, k).wait_recv()
            total = gd[x, yl, c, :, wcols(g)].astype(F32)
            for k in (0, 1, 2):
                total += r1[l, k, :, wcols(g)].astype(F32)
            wgrad_ref[:, wcols(g)] = total

    def direct(l, g):
        return l == 0 and g < 2

    def pair_copy(l, g):
        return remote(
            p1.at[l, (s + l + 1 + yl) % 2, :, wcols(g)], r2.at[l, 0, :, wcols(g)],
            ry_send.at[l, g, 0], ry_recv.at[l, g, 0], pair,
        )

    def cut_copy(l, g):
        return remote(
            p1.at[l, 1 - yl, :, wcols(g)], r2.at[l, 1, :, wcols(g)],
            ry_send.at[l, g, 1], ry_recv.at[l, g, 1], beyond,
        )

    @scoped("reduce_g")
    def reduce_g(l, g):
        @pl.when(s != l)
        def _():
            pair_copy(l, g).wait_recv()
            p1[l, 1 - yl, :, wcols(g)] = (
                p1[l, 1 - yl, :, wcols(g)].astype(F32) + r2[l, 0, :, wcols(g)].astype(F32)
            ).astype(BF16)

        begin("ry", cut_copy(l, g), s != l)

    @scoped("reduce_done")
    def reduce_done(l, g):
        if direct(l, g):
            copies = [
                remote(
                    p1.at[l, 0, :, wcols(g)], r2.at[l, k, :, wcols(g)],
                    ry_send.at[l, g, k], ry_recv.at[l, g, k], yp[k],
                )
                for k in (0, 1, 2)
            ]
        else:
            copies = [pair_copy(l, g), cut_copy(l, g)]

        @pl.when(s == l)
        def _():
            for copy in copies:
                copy.wait_recv()
            total = p1[l, yl, :, wcols(g)].astype(F32)
            for k in range(len(copies)):
                total += r2[l, k, :, wcols(g)].astype(F32)
            wgrad_ref[:, wcols(g)] = total

    def spread_start(event, buf, h):
        mine = buf.at[t, part(h)]
        for k in (1, 2, 3):
            begin("z", remote(mine, mine, z_send.at[event, h, k - 1], z_recv.at[event, h, k - 1], zp[k - 1]))

    @scoped("spread_done")
    def spread_done(event, buf, h):
        for k in (1, 2, 3):
            theirs = buf.at[(t - k + 4) % 4, part(h)]
            remote(theirs, theirs, z_send.at[event, h, k - 1], z_recv.at[event, h, k - 1], zp[k - 1]).wait_recv()

    def sum_copy(event, h, k):
        return remote(
            sbuf.at[(event // 2) % 3, (t + k) % 4, part(h)], rbuf.at[event // 2, k - 1, part(h)],
            z_send.at[event, h, k - 1], z_recv.at[event, h, k - 1], zp[k - 1],
        )

    def sum_start(event, h):
        for k in (1, 2, 3):
            begin(("s", (event // 2) % 3, h), sum_copy(event, h, k))

    @scoped("sum_done")
    def sum_done(event, h):
        for k in (1, 2, 3):
            sum_copy(event, h, k).wait_recv()
        total = sbuf[(event // 2) % 3, t, rows(h)].astype(F32)
        for k in (0, 1, 2):
            total += rbuf[event // 2, k, rows(h)].astype(F32)
        return total

    @scoped("share")
    def share(event, h, lhs, l, c0, n):
        slot = (event // 2) % 3
        flush(("s", slot, h))

        def tile(j, _):
            right = w[l, j, :, :, :, pl.ds(c0, n)].reshape(256, n)
            value = dot_nt(lhs().reshape(4 * HALF, n), right).astype(BF16)
            sbuf[slot, :, rows(h), aligned(j, 256)] = value.reshape(4, HALF, 256)
            return 0

        lax.fori_loop(0, 4, tile, 0)
        sum_start(event, h)

    fills = []

    def fill(count):
        for _ in range(min(count, len(fills))):
            fills.pop(0)()

    def weight_grad(l, parts, lhs_ref, rhs_ref):
        c0, n = REDUCE[parts[0]][0], sum(REDUCE[g][1] for g in parts)

        @scoped("weight_grad")
        def one(step):
            at = (x + step) % 4
            gt_s[...] = lhs_ref[:, :, aligned(at, 256)].reshape(SEQ, 256).T

            def tile(j, _):
                value = dot_nn(gt_s[...], rhs_ref[:, :, aligned(j, 256)].reshape(SEQ, 256))
                gd[at, :, :, :, pl.ds(pl.multiple_of(c0 + j * 256, 256), 256)] = value.astype(
                    BF16
                ).reshape(2, 2, ROWS, 256)
                return 0

            lax.fori_loop(0, n // 256, tile, 0)
            for g in parts:
                begin(("rc", l, g), c_copy(l, g, step))

        for step in (2, 1, 3, 0):
            fills.append(functools.partial(one, step))

    def reduce_all(l, g):
        for step in (2, 1, 3, 0):
            reduce_c(l, g, step)

    def cross_send(index, value, l, local_ref, h):
        @pl.when(s == l)
        def _():
            local_ref[s, rows(h)] = value

        @pl.when(s != l)
        def _():
            xs[index, rows(h)] = value.astype(BF16)

        begin("o", remote(
            xs.at[index, part(h)], xr.at[index, part(h)], o_send.at[index, h], o_recv.at[index, h], across
        ), s != l)

    stages = {
        "c": ((late_c, early_c), c, [mate], 0), "x": ((late_x, early_x), x, xp, 1),
        "y": ((late_y, early_y), y, yp, 4), "z": ((late_z, early_z), t, zp, 7),
    }

    def all_sum(kind, l, stage):
        bufs, _, peers, _ = stages[stage]
        value = bufs[kind][l, 0]
        for k in range(1, len(peers) + 1):
            value = value + bufs[kind][l, k]
        return value

    def all_start(kind, l, stage, before=None):
        bufs, me, peers, at = stages[stage]
        buf = bufs[kind]
        buf[l, me] = (late, early)[kind][l] if before is None else all_sum(kind, l, before)
        for k, peer in enumerate(peers):
            begin("a", remote(
                buf.at[l, me], buf.at[l, me], a_send.at[kind, l, at + k], a_recv.at[kind, l, at + k], peer
            ))

    @scoped("all_wait")
    def all_wait(kind, l, stage):
        bufs, me, peers, at = stages[stage]
        n = len(peers) + 1
        for k, peer in enumerate(peers):
            theirs = bufs[kind].at[l, (me - k - 1 + n) % n]
            remote(theirs, theirs, a_send.at[kind, l, at + k], a_recv.at[kind, l, at + k], peer).wait_recv()

    def all_next(kind, l, stage, following):
        all_wait(kind, l, stage)
        all_start(kind, l, following, stage)

    def small(l, row):
        return pb[l, row:row + 1]

    def norm_one(l, h, hidden):
        normed, unit, inverse = norm_rows(hidden, small(l, GAIN), small(l, OFFSET))
        unit_s[l, 0, rows(h)] = unit
        inv_s[l, 0, rows(h)] = inverse
        g1[l, t, rows(h)] = normed.astype(BF16)
        spread_start(4 * l, g1.at[l], h)
        mid_s[rows(h)] = hidden

    def project(l, h):
        left = g1[l, :, rows(h)].reshape(4 * HALF, D)
        for j in range(3):
            value = dot_nn(left, w[l, :, :, :, :, j * 256:(j + 1) * 256].reshape(D, 256))
            if j != 1:
                value = value + pb[l, QV + j // 2:QV + j // 2 + 1, aligned(t, 256)]
            qkv_s[l, :, rows(h), j * 256:(j + 1) * 256] = value.astype(BF16).reshape(4, HALF, 256)

    def head(l, j, n):
        return qkv_s[l, :, :, j * 256 + n * HD:j * 256 + (n + 1) * HD].reshape(SEQ, HD)

    @scoped("attend")
    def attend(l):
        for pair in range(2):
            mixed = []
            for n in (2 * pair, 2 * pair + 1):
                scores = dot_nt(head(l, 0, n), head(l, 1, n)) * 0.125
                scores = jnp.where(mask_s[...] > 0.5, scores, NEGATIVE)
                shifted = jnp.exp(scores - jnp.max(scores, axis=-1, keepdims=True))
                probs = shifted / jnp.sum(shifted, axis=-1, keepdims=True)
                prob_s[l, n] = probs
                mixed.append(dot_nn(probs.astype(BF16), head(l, 2, n)))
            both = jnp.concatenate(mixed, axis=1).astype(BF16)
            mixed_s[l, :, :, pair * 128:(pair + 1) * 128] = both.reshape(4, ROWS, 128)

    def norm_two(l, h):
        middle = mid_s[rows(h)] + (sum_done(4 * l + 1, h) + small(l, PROJ))
        normed, unit, inverse = norm_rows(middle, small(l, GAIN + 1), small(l, OFFSET + 1))
        unit_s[l, 1, rows(h)] = unit
        inv_s[l, 1, rows(h)] = inverse
        g2[l, t, rows(h)] = normed.astype(BF16)
        spread_start(4 * l + 2, g2.at[l], h)
        mid_s[rows(h)] = middle

    @scoped("up")
    def up(l, h):
        def tile(j, _):
            at = aligned(j, 256)
            before = dot_nn(
                g2[l, :, rows(h)].reshape(4 * HALF, D),
                w[l, :, :, :, :, pl.ds(pl.multiple_of(1024 + j * 256, 256), 256)].reshape(D, 256),
            ) + pb[l, pl.ds(FC + t, 1), at]
            tanh_part = jnp.tanh(GELU_COEF * (before + 0.044715 * before * before * before))
            active = (0.5 * before * (1.0 + tanh_part)).astype(BF16)
            slope = 0.5 * (1.0 + tanh_part) + 0.5 * before * (
                1.0 - tanh_part * tanh_part
            ) * GELU_COEF * (1.0 + 3.0 * 0.044715 * before * before)
            active_s[l, :, rows(h), at] = active.reshape(4, HALF, 256)
            if l == 0:
                slope_s[l, :, rows(h), at] = slope.reshape(4, HALF, 256)
            else:
                grad_before = slope_s[l, :, rows(h), at].reshape(4 * HALF, 256) * slope
                early[l, pl.ds(4 + t, 1), at] += row_sum(grad_before)
                gb_s[:, rows(h), at] = grad_before.astype(BF16).reshape(4, HALF, 256)
            return 0

        lax.fori_loop(0, 4, tile, 0)

    def layer_out(l, h):
        return mid_s[rows(h)] + (sum_done(4 * l + 3, h) + small(l, PROJ + 1))

    def attention_part(l):
        for h in BOTH:
            spread_done(4 * l, g1.at[l], h)
            if h == 0:
                gather_done(l, 0)
            project(l, h)
        gather_c(l, 1)
        attend(l)
        gather_done(l, 1)
        for h in BOTH:
            share(4 * l + 1, h, lambda h=h: mixed_s[l, :, rows(h)], l, 768, 256)

    @scoped("before_up")
    def before_up(l):
        def tile(j, _):
            value = dot_nn(
                gm[l].reshape(SEQ, D),
                w[l, :, :, :, :, pl.ds(pl.multiple_of(2048 + j * 256, 256), 256)].reshape(D, 256),
            )
            slope_s[l, :, :, aligned(j, 256)] = value.reshape(4, ROWS, 256)
            return 0

        lax.fori_loop(0, 4, tile, 0)

    @scoped("down")
    def down(l, h):
        def tile(j, _):
            at = aligned(j, 256)
            grad_before = dot_nn(
                gm[l, :, rows(h)].reshape(4 * HALF, D),
                w[l, :, :, :, :, pl.ds(pl.multiple_of(2048 + j * 256, 256), 256)].reshape(D, 256),
            ) * slope_s[l, :, rows(h), at].reshape(4 * HALF, 256)
            early[l, pl.ds(4 + t, 1), at] += row_sum(grad_before)
            gb_s[:, rows(h), at] = grad_before.astype(BF16).reshape(4, HALF, 256)
            return 0

        lax.fori_loop(0, 4, tile, 0)

    def norm_two_back(l, h):
        grad = sum_done(13 - 4 * l, h)
        unit = unit_s[l, 1, rows(h)]
        early[l, 0:1] += row_sum(grad * unit)
        early[l, 1:2] += row_sum(grad)
        grad_middle = dy_s[rows(h)] + norm_back(grad, unit, inv_s[l, 1, rows(h)], small(l, GAIN + 1))
        dy_s[rows(h)] = grad_middle
        ga[l, t, rows(h)] = grad_middle.astype(BF16)
        spread_start(14 - 4 * l, ga.at[l], h)
        early[l, 2:3] += row_sum(grad_middle)

    def mixed_back(l, h):
        value = dot_nn(
            ga[l, :, rows(h)].reshape(4 * HALF, D), w[l, :, :, :, :, 768:1024].reshape(D, 256)
        )
        gx_s[:, rows(h)] = value.astype(BF16).reshape(4, HALF, 256)

    @scoped("attend_back")
    def attend_back(l):
        for pair in range(2):
            grads = [[], [], []]
            for n in (2 * pair, 2 * pair + 1):
                q, key, value = head(l, 0, n), head(l, 1, n), head(l, 2, n)
                grad_head = gx_s[:, :, n * HD:(n + 1) * HD].reshape(SEQ, HD)
                probs = prob_s[l, n]
                grad_probs = dot_nt(grad_head, value)
                row_dot = jnp.sum(probs * grad_probs, axis=-1, keepdims=True)
                grad_scores = (probs * (grad_probs - row_dot)).astype(BF16)
                grads[0].append(dot_nn(grad_scores, key) * 0.125)
                grads[1].append(dot_tn(grad_scores, q) * 0.125)
                grads[2].append(dot_tn(probs.astype(BF16), grad_head))
            for j in range(3):
                both = jnp.concatenate(grads[j], axis=1)
                gp_s[:, :, j * 256 + pair * 128:j * 256 + (pair + 1) * 128] = both.astype(BF16).reshape(
                    4, ROWS, 128
                )
                if j != 1:
                    total = row_sum(both)
                    for k in BOTH:
                        late[l, 4 + j + k:5 + j + k, aligned((t % 2) * 2 + pair, 128)] = jnp.where(
                            t // 2 == k, total, 0.0
                        )

    def norm_one_back(l, h):
        grad = sum_done(15 - 4 * l, h)
        unit = unit_s[l, 0, rows(h)]
        for row, value in ((0, row_sum(grad * unit)), (2, row_sum(grad))):
            late[l, row:row + 1] += value[:, :512]
            late[l, row + 1:row + 2] += value[:, 512:]
        return dy_s[rows(h)] + norm_back(grad, unit, inv_s[l, 0, rows(h)], small(l, GAIN))

    pb[s, GAIN:GAIN + 2] = gain_ref[...]
    pb[s, OFFSET:OFFSET + 2] = offset_ref[...]
    pb[s, PROJ:PROJ + 2] = proj_ref[...]
    pb[s, QV:QV + 2] = qv_ref[...]
    for k in range(4):
        pb[s, FC + k:FC + k + 1] = fc_ref[:, k * 1024:(k + 1) * 1024]
    pb[s, FC + 4:] = jnp.zeros((SMALL - FC - 4, D), F32)
    for j in range(3):
        w[s, x, yl, c, :, j * 256:(j + 1) * 256] = qkv_ref[j]
    gather_y(0)
    w[s, x, yl, c, :, 768:1024] = wo_ref[...]
    gather_y(1)
    w[s, x, yl, c, :, 2048:] = fc2_ref[...]
    turn_x(5)
    begin("pb", remote(pb.at[s], pb.at[s], o_send.at[4, 0], o_recv.at[4, 0], across))
    w[s, x, yl, c, :, 1024:2048] = fc1_ref[...]
    late[...] = jnp.zeros_like(late)
    early[...] = jnp.zeros_like(early)
    seg_rows = jnp.broadcast_to(seg_ref[s].astype(F32), (SEQ, SEQ))
    seg_cols = seg_rows.T
    places_i = lax.broadcasted_iota(jnp.int32, (SEQ, SEQ), 0)
    places_j = lax.broadcasted_iota(jnp.int32, (SEQ, SEQ), 1)
    mask_s[...] = jnp.where((seg_rows == seg_cols) & (places_i >= places_j), 1.0, 0.0)
    gather_x(0, 0)
    gather_y(2)
    gather_x(0, 1)
    gather_y(3)
    gather_y(4)
    turn_y(5)
    with jax.named_scope("wait_pb"):
        remote(pb.at[1 - s], pb.at[1 - s], o_send.at[4, 0], o_recv.at[4, 0], across).wait_recv()
    for h in BOTH:
        norm_one(0, h, x_ref[s, rows(h)].astype(F32))
    gm[1, t] = cot_ref[s]
    for h in BOTH:
        spread_start(8, gm.at[1], h)
    dy_s[...] = cot_ref[s].astype(F32)
    early[1, 3:4] = row_sum(dy_s[...])
    gather_c(0, 0)
    for g in (2, 3, 4):
        gather_x(0, g)

    attention_part(0)
    gather_c(0, 2)
    gather_x(1, 0)
    gather_x(1, 1)
    for h in BOTH:
        norm_two(0, h)
    gather_c(0, 3)
    gather_c(0, 4)
    turn_c(0, 5)
    for h in BOTH:
        spread_done(2, g2.at[0], h)
        if h == 0:
            gather_done(0, 2)
            gather_done(0, 3)
        up(0, h)
        if h == 0:
            gather_done(0, 4)
            gather_done(0, 5)
        share(3, h, lambda h=h: active_s[0, :, rows(h)], 0, 2048, 1024)
    gather_x(1, 4)
    gather_x(1, 2)
    for h in BOTH:
        hidden = layer_out(0, h)
        norm_one(1, h, hidden.astype(BF16).astype(F32))
        cross_send(0, hidden, 0, out_ref, h)
        if h == 0:
            gather_c(1, 0)
    gather_x(1, 3)
    turn_c(1, 5)

    attention_part(1)
    for h in BOTH:
        spread_done(8, gm.at[1], h)
    gather_c(1, 4)
    gather_done(1, 5)
    gather_c(1, 2)
    gather_done(1, 4)
    before_up(1)
    for h in BOTH:
        norm_two(1, h)
    gather_c(1, 3)
    weight_grad(1, (3, 4), gm.at[1], active_s.at[1])
    weight_grad(1, (2,), g2.at[1], gb_s)
    for h in BOTH:
        spread_done(6, g2.at[1], h)
        if h == 0:
            gather_done(1, 2)
            gather_done(1, 3)
        up(1, h)
        share(9, h, lambda h=h: gb_s[:, rows(h)], 1, 1024, 1024)
    fill(4)
    norm_two_back(1, 0)
    fill(2)
    norm_two_back(1, 1)
    fill(1)
    reduce_all(1, 3)
    reduce_all(1, 4)
    fill(1)
    share(7, 0, lambda: active_s[1, :, rows(0)], 1, 2048, 1024)
    spread_done(10, ga.at[1], 0)
    mixed_back(1, 0)
    share(7, 1, lambda: active_s[1, :, rows(1)], 1, 2048, 1024)
    spread_done(10, ga.at[1], 1)
    mixed_back(1, 1)
    attend_back(1)
    for h in BOTH:
        share(11, h, lambda h=h: gp_s[:, rows(h)], 1, 0, 768)
    reduce_all(1, 2)
    reduce_f(1, 3)
    reduce_f(1, 4)
    weight_grad(1, (0,), g1.at[1], gp_s)
    weight_grad(1, (1,), ga.at[1], mixed_s.at[1])
    fill(8)

    def pass_grad(h):
        grad = norm_one_back(1, h).astype(BF16)
        gm[0, t, rows(h)] = grad
        spread_start(12, gm.at[0], h)
        dy_s[rows(h)] = grad.astype(F32)
        cross_send(3, grad.astype(F32), 1, grad_ref, h)

    pass_grad(0)
    for h in BOTH:
        hidden = layer_out(1, h)
        cross_send(2, hidden, 1, out_ref, h)
    pass_grad(1)
    reduce_f(1, 2)
    reduce_all(1, 0)
    early[0, 3:4] = row_sum(dy_s[...])
    for kind in BOTH:
        all_start(kind, 1, "c")

    for h in BOTH:
        spread_done(12, gm.at[0], h)
        down(0, h)
        share(13, h, lambda h=h: gb_s[:, rows(h)], 0, 1024, 1024)
    for kind in BOTH:
        all_next(kind, 1, "c", "y")
    reduce_all(1, 1)
    reduce_y(1, 3)
    reduce_y(1, 4)
    for g in (4, 3, 2):
        flush(("rc", 1, g))
        flush(("rx", 1, g))
    weight_grad(0, (3, 4), gm.at[0], active_s.at[0])
    weight_grad(0, (2,), g2.at[0], gb_s)
    fill(4)
    reduce_f(1, 0)
    norm_two_back(0, 0)
    reduce_y(1, 2)
    fill(2)
    norm_two_back(0, 1)
    all_start(1, 0, "c")
    reduce_f(1, 1)
    reduce_all(0, 4)
    reduce_all(0, 3)
    fill(2)
    reduce_g(1, 3)
    reduce_g(1, 4)
    spread_done(14, ga.at[0], 0)
    mixed_back(0, 0)
    reduce_g(1, 2)
    reduce_y(1, 0)
    for kind in BOTH:
        all_next(kind, 1, "y", "x")
    spread_done(14, ga.at[0], 1)
    mixed_back(0, 1)
    reduce_all(0, 2)
    all_next(1, 0, "c", "y")
    attend_back(0)
    for h in BOTH:
        share(15, h, lambda h=h: gp_s[:, rows(h)], 0, 0, 768)
    reduce_y(1, 1)
    for g in (1, 0):
        flush(("rc", 1, g))
        flush(("rx", 1, g))
    weight_grad(0, (1,), ga.at[0], mixed_s.at[0])
    fill(4)
    wide_y(0, 4)
    reduce_f(0, 3)
    reduce_g(1, 0)
    weight_grad(0, (0,), g1.at[0], gp_s)
    fill(3)
    reduce_all(0, 1)
    fill(1)
    all_next(1, 0, "y", "x")
    reduce_c(0, 0, 2)
    reduce_f(0, 2)
    for step in (1, 3, 0):
        reduce_c(0, 0, step)
    reduce_g(1, 1)
    cross_send(1, norm_one_back(0, 0), 0, grad_ref, 0)
    for kind in BOTH:
        all_next(kind, 1, "x", "z")
    cross_send(1, norm_one_back(0, 1), 0, grad_ref, 1)
    all_start(0, 0, "c")
    all_next(0, 0, "c", "z")
    reduce_y(0, 3)
    all_next(0, 0, "z", "y")
    reduce_f(0, 0)
    reduce_f(0, 1)
    all_next(1, 0, "x", "z")
    reduce_y(0, 2)
    all_next(0, 0, "y", "x")
    wide_x(0, 4)
    reduce_g(0, 3)
    reduce_y(0, 0)
    reduce_y(0, 1)
    reduce_g(0, 2)
    for g in (4, 3, 2, 1, 0):
        reduce_done(1, g)
    for kind in BOTH:
        all_wait(kind, 1, "z")
    all_wait(0, 0, "x")
    all_wait(1, 0, "z")
    for kind, ref in ((0, late_ref), (1, early_ref)):
        ref[...] = jnp.where(s == 0, all_sum(kind, 0, "zx"[1 - kind]), all_sum(kind, 1, "z"))
    for ref, pairs in ((out_ref, (0, 2)), (grad_ref, (1, 3))):
        for h in BOTH:
            first, second = [
                remote(
                    xs.at[index, part(h)], xr.at[index, part(h)], o_send.at[index, h], o_recv.at[index, h], across
                )
                for index in pairs
            ]
            pl.when(s == 0)(first.wait_recv)
            pl.when(s == 1)(second.wait_recv)

        @pl.when(s == 0)
        def _():
            ref[1 - s] = xr[pairs[0]].astype(F32)

        @pl.when(s == 1)
        def _():
            ref[1 - s] = xr[pairs[1]].astype(F32)

    wide_done(0, 4)
    for g in (3, 2, 1, 0):
        reduce_done(0, g)
    for key in list(pending):
        flush(key)


def finish(
    out_ref, grad_ref, wgrad_ref, late_ref, early_ref,
    outs, grads, qkv, out, fc1, fc2, gain, offset, qv, proj, fc,
):
    outs[0] = out_ref[...]
    grads[0] = grad_ref[...]
    for j in range(3):
        qkv[0, j] = wgrad_ref[:, j * 256:(j + 1) * 256]
    out[0] = wgrad_ref[:, 768:1024]
    fc1[0] = wgrad_ref[:, 1024:2048]
    fc2[0] = wgrad_ref[:, 2048:]
    for ref, row, other in ((gain, 0, 0), (offset, 2, 1)):
        for k in BOTH:
            ref[0, 0:1, k * 512:(k + 1) * 512] = late_ref[row + k:row + k + 1]
        ref[0, 1:2] = early_ref[other:other + 1]
    for row in BOTH:
        for k in BOTH:
            at = 4 + 2 * row + k
            qv[0, row:row + 1, k * 512:(k + 1) * 512] = late_ref[at:at + 1]
    proj[0] = early_ref[2:4]
    for k in range(4):
        fc[:, k * 1024:(k + 1) * 1024] = early_ref[4 + k:5 + k]


def fused(*args):
    vmem = pl.BlockSpec(memory_space=pltpu.VMEM)
    dma = pltpu.SemaphoreType.DMA
    scratch = [
        pltpu.VMEM((2, 4, 2, 2, ROWS, WIDE), BF16),
        pltpu.VMEM((4, 2, 2, ROWS, WIDE), BF16),
        pltpu.VMEM((2, 4, 2, ROWS, WIDE), BF16),
        pltpu.VMEM((2, 6, ROWS, WIDE), BF16),
        pltpu.VMEM((2, 3, ROWS, WIDE), BF16),
        pltpu.VMEM((2, 4, ROWS, 512), BF16),
        pltpu.VMEM((2, 2, ROWS, WIDE), BF16),
        pltpu.VMEM((2, SMALL, D), F32),
        pltpu.VMEM((2, 4, ROWS, D), BF16),
        pltpu.VMEM((2, 4, ROWS, D), BF16),
        pltpu.VMEM((2, 4, ROWS, D), BF16),
        pltpu.VMEM((2, 4, ROWS, D), BF16),
        pltpu.VMEM((3, 4, ROWS, D), BF16),
        pltpu.VMEM((8, 3, ROWS, D), BF16),
        pltpu.VMEM((2, 4, ROWS, 768), BF16),
        pltpu.VMEM((2, 4, SEQ, SEQ), F32),
        pltpu.VMEM((2, 4, ROWS, 256), BF16),
        pltpu.VMEM((2, 4, ROWS, D), BF16),
        pltpu.VMEM((2, 4, ROWS, D), F32),
        pltpu.VMEM((2, 2, ROWS, D), F32),
        pltpu.VMEM((2, 2, ROWS, 1), F32),
        pltpu.VMEM((ROWS, D), F32),
        pltpu.VMEM((4, ROWS, D), BF16),
        pltpu.VMEM((4, ROWS, 768), BF16),
        pltpu.VMEM((4, ROWS, 256), BF16),
        pltpu.VMEM((256, SEQ), BF16),
        pltpu.VMEM((SEQ, SEQ), F32),
        pltpu.VMEM((ROWS, D), F32),
        pltpu.VMEM((4, ROWS, D), BF16),
        pltpu.VMEM((4, ROWS, D), BF16),
        pltpu.VMEM((2, 8, 512), F32),
        pltpu.VMEM((2, 8, D), F32),
    ]
    for width in (512, D):
        scratch += [pltpu.VMEM((2, n, 8, width), F32) for n in (2, 4, 4, 4)]
    scratch += [
        dma((16, 2, 3)), dma((16, 2, 3)),
        dma((6, 3)), dma((2, 6, 3)),
        dma((2, 6, 3)), dma((2, 6, 3)),
        dma((2, 6)), dma((2, 6)),
        dma((2, 5, 4)), dma((2, 5, 4)),
        dma((2, 5, 6)), dma((2, 5, 6)),
        dma((2, 5, 3)), dma((2, 5, 3)),
        dma((5, 2)), dma((5, 2)),
        dma((2, 2, 10)), dma((2, 2, 10)),
    ]
    sums = pl.pallas_call(
        kernel,
        out_shape=(
            jax.ShapeDtypeStruct((2, ROWS, D), F32),
            jax.ShapeDtypeStruct((2, ROWS, D), F32),
            jax.ShapeDtypeStruct((ROWS, WIDE), F32),
            jax.ShapeDtypeStruct((8, 512), F32),
            jax.ShapeDtypeStruct((8, D), F32),
        ),
        in_specs=[vmem] * 12,
        out_specs=(vmem,) * 5,
        scratch_shapes=scratch,
        compiler_params=pltpu.CompilerParams(
            collective_id=0, has_side_effects=True, vmem_limit_bytes=62 * 2**20
        ),
    )(*args)
    return pl.pallas_call(
        finish,
        out_shape=(
            jax.ShapeDtypeStruct((1, 2, ROWS, D), F32),
            jax.ShapeDtypeStruct((1, 2, ROWS, D), F32),
            jax.ShapeDtypeStruct((1, 3, ROWS, 256), F32),
            jax.ShapeDtypeStruct((1, ROWS, 256), F32),
            jax.ShapeDtypeStruct((1, ROWS, 1024), F32),
            jax.ShapeDtypeStruct((1, ROWS, 1024), F32),
            jax.ShapeDtypeStruct((1, 2, D), F32),
            jax.ShapeDtypeStruct((1, 2, D), F32),
            jax.ShapeDtypeStruct((1, 2, D), F32),
            jax.ShapeDtypeStruct((1, 2, D), F32),
            jax.ShapeDtypeStruct((1, FF), F32),
        ),
        in_specs=[vmem] * 5,
        out_specs=(vmem,) * 11,
    )(*sums)


def local(
    inputs, cotangent, segments, qkv_weight, out_weight, fc1_weight, fc2_weight,
    ln_gains, ln_biases, qv_bias, proj_biases, fc_bias,
):
    outs, grads, qkv, out, fc1, fc2, gain, offset, qv, proj, fc = fused(
        inputs, cotangent, segments,
        jnp.transpose(qkv_weight[0], (1, 0, 2)), out_weight[0].T, fc1_weight[0], fc2_weight[0].T,
        ln_gains[0], ln_biases[0], qv_bias[0], proj_biases[0], fc_bias,
    )
    return (
        outs, grads, jnp.transpose(qkv, (0, 2, 1, 3)), jnp.transpose(out, (0, 2, 1)), fc1,
        jnp.transpose(fc2, (0, 2, 1)), gain, offset, qv, proj, fc,
    )


def solution(mesh):
    in_specs = (
        P(None, ("dp", "tensor"), None),
        P(None, ("dp", "tensor"), None),
        P(None, "dp", None),
        P("section", "dp", None, "tensor"),
        P("section", "tensor", "dp"),
        P("section", "dp", "tensor"),
        P("section", "tensor", "dp"),
        P("section", None, None),
        P("section", None, None),
        P("section", None, None),
        P("section", None, None),
        P("section", None),
    )
    out_specs = (
        P("section", None, ("dp", "tensor"), None),
        P("section", None, ("dp", "tensor"), None),
        P("section", "dp", None, "tensor"),
        P("section", "tensor", "dp"),
        P("section", "dp", "tensor"),
        P("section", "tensor", "dp"),
        P("section", None, None),
        P("section", None, None),
        P("section", None, None),
        P("section", None, None),
        P("section", None),
    )
    return jax.shard_map(local, mesh=mesh, in_specs=in_specs, out_specs=out_specs, check_vma=False)
```
